512 devices in a mesh: section: 8 (over x, z_hi), tp: 64 (over z_lo, y, core).
Axes of the slice: x: 4, y: 4, z: 16 (z_hi: 2, z_lo: 8; z = z_hi * 8 + z_lo), core: 2. Of those that a mesh axis runs over, the one named last changes fastest.
Arguments:
- residual: bfloat16 [8, 512, 8192], P('section', 'tp'), may hold values from -300 to 300
- norm_gain: float32 [8, 8192], P('section'), may hold values from 0.1 to 1.9
- query_weight: bfloat16 [8, 8192, 8192], P('section', None, 'tp'), may hold values from -0.0625 to 0.0625
- kv_weight: bfloat16 [8, 8192, 2048], P('section', None, 'tp'), may hold values from -0.0625 to 0.0625
- resident_cache: bfloat16 [8, 8, 512, 256], P('section'), may hold values from -500 to 500
- block_start: int32 [8], P('section'), may hold values from 512 to 130560
- decode_owner: int32 [8, 8], P('section'), may hold values from 0 to 63
Outputs:
- attn_heads: bfloat16 [8, 512, 8192], P('section', None, 'tp')
- decode_kv: bfloat16 [8, 512, 8, 256], P('section', 'tp')
The draws below stay inside these ranges and needn't reach their ends.
All inputs are finite; a program needn't handle non-finite values.
Results may differ from the reference program's by a relative error of at most 0.025.
Values may be sent and summed in bfloat16 or wider, within the bound.
No kernel may reach another device: no remote copies, remote signals or barrier semaphores. Data moves between devices by JAX's collectives and lax.ppermute only.
A program may use at most 64 MiB of HBM per device.

```python
import math
import jax
import jax.numpy as jnp
from jax import lax

D = 8192
HEADS = 64
KV_HEADS = 8
HEAD_DIM = 128
NEW_TOKENS = 512
RESIDENT = 512
SECTIONS = 8
N_TP = 64


def draw_residual(key, part):
    key = jax.random.fold_in(key, 11)
    base_key, row_key, col_key = jax.random.split(key, 3)
    shape = (SECTIONS, NEW_TOKENS, D)
    row_scale = jnp.exp(jax.random.uniform(row_key, (SECTIONS, NEW_TOKENS, 1), jnp.float32) * math.log(10.0))
    col_scale = jnp.exp(jax.random.uniform(col_key, (1, 1, D), jnp.float32) * math.log(10.0))
    noise = jnp.clip(jax.random.normal(base_key, shape, jnp.float32), -5.0, 5.0)
    return (0.3 * noise * row_scale * col_scale).astype(jnp.bfloat16)


def draw_resident_cache(key, part):
    key = jax.random.fold_in(key, 23)
    base_key = jax.random.fold_in(key, 0)
    shape = (SECTIONS, KV_HEADS, RESIDENT, 2 * HEAD_DIM)
    entries = jnp.clip(jax.random.normal(base_key, shape, jnp.float32), -6.0, 6.0)
    return entries.astype(jnp.bfloat16)


def plant(array, own_key, smallest, largest):
    longest = array.shape.index(max(array.shape))
    spots = []
    for shift in (0, 1):
        where = [jax.random.randint(jax.random.fold_in(own_key, axis), (), 0, length) for axis, length in enumerate(array.shape)]
        where[longest] = (where[longest] + shift) % array.shape[longest]
        spots.append(tuple(where))
    return array.at[spots[0]].set(smallest).at[spots[1]].set(largest)


def level_of(key, extent, cuts, smallest, largest):
    def one(position, blocks):
        draws = jax.random.uniform(jax.random.fold_in(jax.random.fold_in(key, 6), position), (blocks,), jnp.float32, smallest / len(cuts), largest / len(cuts))
        return jnp.repeat(jnp.exp(draws), extent[position] // blocks).reshape((-1,) + (1,) * (len(extent) - position - 1))

    factor_of = one(*cuts[0])
    for cut in cuts[1:]:
        factor_of = factor_of * one(*cut)
    return factor_of


def bell_draw(key, shape, scale, bound, cuts=(), kind=jnp.bfloat16):
    array = jax.random.normal(key, shape, jnp.float32) * scale
    if len(cuts) > 0:
        array = level_of(key, shape, cuts, -0.22, 0.18) * array
    return jnp.clip(array, min=-bound, max=bound).astype(kind)


def setup_inputs(seed: int = 0) -> dict:
    keys = jax.random.split(jax.random.key(seed), 8)
    return {
        "residual": draw_residual(jax.random.fold_in(keys[7], 71), 0),
        "norm_gain": jnp.clip(1.0 + 0.18 * jax.random.normal(keys[1], (SECTIONS, D), jnp.float32), 0.1, 1.9),
        "query_weight": bell_draw(keys[2], (SECTIONS, D, HEADS * HEAD_DIM), D ** -0.5, 0.0625, ((0, 8), (2, 64))),
        "kv_weight": bell_draw(keys[3], (SECTIONS, D, 2 * KV_HEADS * HEAD_DIM), D ** -0.5, 0.0625, ((0, 8), (2, 64))),
        "resident_cache": draw_resident_cache(jax.random.fold_in(keys[7], 71), 0),
        "block_start": plant(jax.random.randint(keys[5], (SECTIONS,), RESIDENT, 131073 - NEW_TOKENS), jax.random.fold_in(keys[5], 1), RESIDENT, (131073 - NEW_TOKENS) - 1).astype(jnp.int32),
        "decode_owner": plant(jax.random.randint(keys[6], (SECTIONS, KV_HEADS), 0, N_TP), jax.random.fold_in(keys[6], 1), 0, N_TP - 1).astype(jnp.int32),
    }


rope_base = 500000.0
norm_eps = 1e-05
masked_score = -1e+30

def frequencies(head_dim):
    half_dim = head_dim // 2
    base_freqs = jnp.exp(jnp.arange(half_dim, dtype=jnp.float32) * (-2.0 * math.log(rope_base) / head_dim))
    wavelength = 2.0 * math.pi / base_freqs
    smooth = (8192.0 / wavelength - 1.0) / 3.0
    blended = (1.0 - smooth) * base_freqs / 8.0 + smooth * base_freqs
    return jnp.where(wavelength < 2048.0, base_freqs, jnp.where(wavelength > 8192.0, base_freqs / 8.0, blended))

def rotate(values, positions):
    half_dim = values.shape[-1] // 2
    freqs_table = frequencies(values.shape[-1])
    angles = positions.astype(jnp.float32)[:, None] * freqs_table[None, :]
    cosine = jnp.cos(angles)[:, None, :]
    sine_part = jnp.sin(angles)[:, None, :]
    first_half = values[..., :half_dim]
    second_half = values[..., half_dim:]
    return jnp.concatenate([first_half * cosine - second_half * sine_part, second_half * cosine + first_half * sine_part], axis=-1)

def normalize(rows_in, norm_scale):
    widened = rows_in.astype(jnp.float32)
    scale_row = lax.rsqrt(lax.optimization_barrier(jnp.mean(widened * widened, axis=-1, keepdims=True)) + norm_eps)
    return (widened * scale_row * norm_scale).astype(jnp.bfloat16)

def reference(residual, norm_gain, query_weight, kv_weight, resident_cache, block_start, decode_owner):
    arriving = jnp.roll(residual, 1, axis=0)
    group_size = HEADS // KV_HEADS
    block_rows = NEW_TOKENS // N_TP
    token_ids = jnp.arange(NEW_TOKENS, dtype=jnp.int32)
    allowed = jnp.arange(RESIDENT + NEW_TOKENS, dtype=jnp.int32)[None, :] <= RESIDENT + token_ids[:, None]
    device_ids = jnp.arange(N_TP, dtype=jnp.int32)
    head_ids = jnp.arange(KV_HEADS, dtype=jnp.int32)
    head_outputs = []
    decode_blocks = []
    for section_index in range(SECTIONS):
        normed = normalize(arriving[section_index], norm_gain[section_index])
        positions = block_start[section_index] + token_ids
        query_rows = jnp.dot(normed, query_weight[section_index], preferred_element_type=jnp.float32)
        query_rows = query_rows.reshape(NEW_TOKENS, HEADS, HEAD_DIM)
        query_rows = (rotate(query_rows, positions) * HEAD_DIM ** (-0.5)).astype(jnp.bfloat16)
        raw_kv = jnp.dot(normed, kv_weight[section_index], preferred_element_type=jnp.float32).astype(jnp.bfloat16)
        raw_kv = raw_kv.reshape(NEW_TOKENS, KV_HEADS, 2 * HEAD_DIM)
        new_keys = rotate(raw_kv[:, :, :HEAD_DIM].astype(jnp.float32), positions).astype(jnp.bfloat16)
        new_kv = jnp.concatenate([new_keys, raw_kv[:, :, HEAD_DIM:]], axis=2)
        resident = resident_cache[section_index]
        key_rows = jnp.concatenate([resident[:, :, :HEAD_DIM], jnp.transpose(new_kv[:, :, :HEAD_DIM], (1, 0, 2))], axis=1)
        value_rows = jnp.concatenate([resident[:, :, HEAD_DIM:], jnp.transpose(new_kv[:, :, HEAD_DIM:], (1, 0, 2))], axis=1)
        grouped = query_rows.reshape(NEW_TOKENS, KV_HEADS, group_size, HEAD_DIM).astype(jnp.float32)
        scores = jnp.einsum('tkgd,ksd->kgts', grouped, key_rows.astype(jnp.float32), precision=lax.Precision.HIGHEST)
        scores = jnp.where(allowed[None, None], scores, masked_score)
        row_max = lax.optimization_barrier(jnp.max(scores, axis=3, keepdims=True))
        weights = jnp.exp(scores - row_max)
        probabilities = (weights / lax.optimization_barrier(jnp.sum(weights, axis=3, keepdims=True))).astype(jnp.bfloat16)
        attended = jnp.einsum('kgts,ksd->tkgd', probabilities.astype(jnp.float32), value_rows.astype(jnp.float32), precision=lax.Precision.HIGHEST)
        head_outputs.append(attended.reshape(NEW_TOKENS, HEADS * HEAD_DIM).astype(jnp.bfloat16))
        blocks = (device_ids[:, None] - decode_owner[section_index][None, :]) % N_TP
        row_ids = blocks[:, :, None] * block_rows + jnp.arange(block_rows, dtype=jnp.int32)[None, None, :]
        picked = new_kv[row_ids, head_ids[None, :, None]]
        decode_blocks.append(jnp.transpose(picked, (0, 2, 1, 3)).reshape(NEW_TOKENS, KV_HEADS, 2 * HEAD_DIM))
    return (jnp.stack(head_outputs), jnp.stack(decode_blocks))
```

```python
import math

import jax
import jax.numpy as jnp
from jax import lax
from jax.experimental import pallas as pl
from jax.experimental.pallas import tpu as pltpu
from jax.sharding import Mesh, PartitionSpec as P

BF = jnp.bfloat16
F32 = jnp.float32
rope_base = 500000.0
norm_eps = 1e-05
masked_score = -1e30

NZ, NY = 8, 4
ROWS = 16
TOKENS = 512
HD = 128


def frequencies(head_dim):
    half_dim = head_dim // 2
    base_freqs = jnp.exp(
        jnp.arange(half_dim, dtype=F32) * (-2.0 * math.log(rope_base) / head_dim)
    )
    wavelength = 2.0 * math.pi / base_freqs
    smooth = (8192.0 / wavelength - 1.0) / 3.0
    blended = (1.0 - smooth) * base_freqs / 8.0 + smooth * base_freqs
    return jnp.where(
        wavelength < 2048.0, base_freqs, jnp.where(wavelength > 8192.0, base_freqs / 8.0, blended)
    )


def along_y(value, k):
    return lax.ppermute(value, "y", [((i + k) % NY, i) for i in range(NY)])


def across_z(value, k):
    return lax.ppermute(value, "z", [(i, i ^ k) for i in range(NZ)])


def swap_core(value):
    return lax.ppermute(value, "c", [(0, 1), (1, 0)])


def place(slot, z0, y0):
    return ((z0 ^ (slot >> 2)) << 2) | ((y0 + (slot & 3)) & 3)


def tokens_of(row, z0, y0):
    return place(row >> 4, z0, y0) * ROWS + (row & 15)


def project_kernel(*refs):
    pieces = refs[:16]
    wq, wkv, own, send, x = refs[16:]
    for b in range(4):
        for k in range(4):
            for part in range(2):
                slot = (b + 4 * part) * 4 + k
                x[slot * ROWS : (slot + 1) * ROWS, :] = pieces[b * 4 + k][part]
    kv = lax.dot_general(
        x[...], wkv[...], (((1,), (1,)), ((), ())), preferred_element_type=F32
    )
    own[:, HD:] = kv
    send[:, HD:] = kv.astype(BF)
    q = jnp.dot(x[...], wq[...], preferred_element_type=F32)
    own[:, :HD] = q[:, :HD]
    send[:, :HD] = q[:, HD:].astype(BF)


def turn(v, cosine, sine):
    return v * cosine + pltpu.roll(v, HD // 2, 1) * sine


def kv_kernel(where, owner, own, got, cosine, sine, keys, values, blocks, held):
    z0, y0, c0 = where[0], where[1], where[2]
    raw = (own[:, HD:] + got[:, HD:].astype(F32)).astype(BF)
    k = turn(raw[:, :HD].astype(F32), cosine[...], sine[...]).astype(BF)
    v = raw[:, HD:]
    keys[...] = k
    values[...] = v
    for slot in range(32):
        to = pl.multiple_of(place(slot, z0, y0) * ROWS, ROWS)
        span = slice(slot * ROWS, (slot + 1) * ROWS)
        held[pl.ds(to, ROWS), :HD] = k[span].astype(F32)
        held[pl.ds(to, ROWS), HD:] = v[span].astype(F32)
    first = y0 * 2 + c0 - owner[z0] + 64
    for z in range(NZ):
        block = (first + z * 8) & 63
        blocks[z] = held[pl.ds(pl.multiple_of(block * 8, 8), 8), :].astype(BF)


def attend_kernel(where, own, got, cosine, sine, keys, values, resident, out):
    z0, y0 = where[0], where[1]
    q = own[:, :HD] + got[:, :HD].astype(F32)
    q = (turn(q, cosine[...], sine[...]) * HD ** (-0.5)).astype(BF)
    nt = (((1,), (1,)), ((), ()))
    old = lax.dot_general(q, resident[:, :HD], nt, preferred_element_type=F32)
    new = lax.dot_general(q, keys[...], nt, preferred_element_type=F32)
    token_q = tokens_of(lax.broadcasted_iota(jnp.int32, (TOKENS, 1), 0), z0, y0)
    token_k = tokens_of(lax.broadcasted_iota(jnp.int32, (1, TOKENS), 1), z0, y0)
    new = jnp.where(token_k <= token_q, new, masked_score)
    top = jnp.maximum(
        jnp.max(old, axis=1, keepdims=True), jnp.max(new, axis=1, keepdims=True)
    )
    old = jnp.exp(old - top)
    new = jnp.exp(new - top)
    total = jnp.sum(old, axis=1, keepdims=True) + jnp.sum(new, axis=1, keepdims=True)
    scale = 1.0 / total
    att = jnp.dot((old * scale).astype(BF), resident[:, HD:], preferred_element_type=F32)
    att = att + jnp.dot((new * scale).astype(BF), values[...], preferred_element_type=F32)
    att = att.astype(BF)
    for slot in range(32):
        to = pl.multiple_of(place(slot, z0, y0) * ROWS, ROWS)
        out[pl.ds(to, ROWS), :] = att[slot * ROWS : (slot + 1) * ROWS]


def kv_weight_kernel(where, gain, mine, one, two, three, out):
    y0 = where[1]
    for k, ref in enumerate((mine, one, two, three)):
        to = pl.multiple_of(((y0 + k) & 3) * 64, 64)
        out[pl.ds(to, 64), :] = (ref[...].astype(F32) * gain[...]).astype(BF)


VMEM = pl.BlockSpec(memory_space=pltpu.VMEM)
SMEM = pl.BlockSpec(memory_space=pltpu.SMEM)


def call(kernel, shapes, specs, scratch=(), flops=0, moved=0, exps=0):
    return pl.pallas_call(
        kernel,
        out_shape=shapes,
        in_specs=specs,
        out_specs=jax.tree.map(lambda _: VMEM, shapes),
        scratch_shapes=scratch,
        compiler_params=pltpu.CompilerParams(vmem_limit_bytes=40 * 2**20),
        cost_estimate=pl.CostEstimate(flops=flops, bytes_accessed=moved, transcendentals=exps),
    )


def shaped(*shape, dtype=BF):
    return jax.ShapeDtypeStruct(shape, dtype)


def body(residual, norm_gain, query_weight, kv_weight, resident_cache, block_start, decode_owner):
    z0, y0, c0 = (lax.axis_index(a).astype(jnp.int32) for a in ("z", "y", "c"))
    width = residual.shape[2]
    half = width // 2
    where = jnp.stack([z0, y0, c0])

    widened = residual[0].astype(F32)
    scale_row = lax.rsqrt(jnp.mean(widened * widened, axis=-1, keepdims=True) + norm_eps)
    rows = (widened * scale_row).astype(BF)
    kept = lax.dynamic_slice_in_dim(rows, c0 * half, half, 1)
    crossed = lax.dynamic_slice_in_dim(rows, (1 - c0) * half, half, 1)
    sections = lax.axis_size("s")
    straight = [(s * 2 + c, (s + 1) % sections * 2 + c) for s in range(sections) for c in (0, 1)]
    across = [(s * 2 + c, (s + 1) % sections * 2 + 1 - c) for s in range(sections) for c in (0, 1)]
    same = lax.ppermute(kept, ("s", "c"), straight)
    other = lax.ppermute(crossed, ("s", "c"), across)
    piece = jnp.where(c0 == 0, jnp.stack([same, other]), jnp.stack([other, same]))
    piece = piece.reshape(1, ROWS, half)

    gain = lax.dynamic_slice_in_dim(norm_gain[0], c0 * half, half, 0)
    wq_mine = lax.dynamic_slice_in_dim(query_weight[0], c0 * half, half, 0)
    wq_given = lax.dynamic_slice_in_dim(query_weight[0], (1 - c0) * half, half, 0)
    wq_got = swap_core(wq_given)
    wq = jnp.concatenate([wq_mine, wq_got], axis=1)
    wq = (wq.astype(F32) * gain[:, None]).astype(BF)
    wkv_t = kv_weight[0].T
    kv_mine = lax.dynamic_slice_in_dim(wkv_t, c0 * half, half, 1)
    kv_given = lax.dynamic_slice_in_dim(wkv_t, (1 - c0) * half, half, 1)
    kv_got = swap_core(kv_given)
    kv_chip = jnp.where(
        c0 == 0, jnp.concatenate([kv_mine, kv_got]), jnp.concatenate([kv_got, kv_mine])
    )
    kv_others = [along_y(kv_chip, k) for k in (1, 2, 3)]
    wkv = call(kv_weight_kernel, shaped(256, half), [SMEM] + [VMEM] * 5, moved=2**22)(
        where, gain[None], kv_chip, *kv_others
    )

    pair = jnp.concatenate([piece, across_z(piece, 4)])
    groups = [pair] + [across_z(pair, k) for k in (1, 2, 3)]
    pieces = [p if k == 0 else along_y(p, k) for p in groups for k in range(NY)]

    tokens = tokens_of(jnp.arange(TOKENS, dtype=jnp.int32), z0, y0)
    angles = (block_start[0] + tokens).astype(F32)[:, None] * frequencies(HD)[None, :]
    cosine, sine = jnp.cos(angles), jnp.sin(angles)
    cosine = jnp.concatenate([cosine, cosine], axis=1)
    sine = jnp.concatenate([-sine, sine], axis=1)

    own, send = call(
        project_kernel,
        (shaped(TOKENS, 3 * HD, dtype=F32), shaped(TOKENS, 3 * HD)),
        [VMEM] * 18,
        scratch=[pltpu.VMEM((TOKENS, half), BF)],
        flops=2 * TOKENS * half * 512,
        moved=9 * 2**20,
    )(*pieces, wq, wkv)
    got = swap_core(send)
    keys, values, blocks = call(
        kv_kernel,
        (shaped(TOKENS, HD), shaped(TOKENS, HD), shaped(NZ, 8, 2 * HD)),
        [SMEM, SMEM] + [VMEM] * 4,
        scratch=[pltpu.VMEM((TOKENS, 2 * HD), F32)],
        moved=2**21,
    )(where, decode_owner[0], own, got, cosine, sine)
    spread = lax.all_to_all(blocks, "z", 0, 0)
    decode_kv = jnp.transpose(spread, (1, 0, 2))[None]
    resident = lax.dynamic_index_in_dim(resident_cache[0], z0, 0, keepdims=False)
    attn = call(
        attend_kernel,
        shaped(TOKENS, HD),
        [SMEM] + [VMEM] * 7,
        flops=4 * TOKENS * 1024 * HD,
        moved=2**21,
        exps=TOKENS * 1024,
    )(where, own, got, cosine, sine, keys, values, resident)
    return attn[None], decode_kv


def solution(mesh):
    sections = mesh.shape["section"]
    fine = Mesh(mesh.devices.reshape(sections, NZ, NY, 2), ("s", "z", "y", "c"))
    tp = ("z", "y", "c")
    return jax.shard_map(
        body,
        mesh=fine,
        in_specs=(
            P("s", tp, None),
            P("s", None),
            P("s", None, tp),
            P("s", None, tp),
            P("s", None, None, None),
            P("s"),
            P("s", None),
        ),
        out_specs=(P("s", None, tp), P("s", tp, None, None)),
        check_vma=False,
    )
```

```python
import math

import jax
import jax.numpy as jnp
from jax import lax
from jax.experimental import pallas as pl
from jax.experimental.pallas import tpu as pltpu
from jax.sharding import Mesh, PartitionSpec as P

BF = jnp.bfloat16
F32 = jnp.float32
rope_base = 500000.0
norm_eps = 1e-05
masked_score = -1e30

NZ, NY = 8, 4
ROWS = 16
TOKENS = 512
HD = 128


def frequencies(head_dim):
    half_dim = head_dim // 2
    base_freqs = jnp.exp(
        jnp.arange(half_dim, dtype=F32) * (-2.0 * math.log(rope_base) / head_dim)
    )
    wavelength = 2.0 * math.pi / base_freqs
    smooth = (8192.0 / wavelength - 1.0) / 3.0
    blended = (1.0 - smooth) * base_freqs / 8.0 + smooth * base_freqs
    return jnp.where(
        wavelength < 2048.0, base_freqs, jnp.where(wavelength > 8192.0, base_freqs / 8.0, blended)
    )


def along_y(value, k):
    return lax.ppermute(value, "y", [((i + k) % NY, i) for i in range(NY)])


def across_z(value, k):
    return lax.ppermute(value, "z", [(i, i ^ k) for i in range(NZ)])


def swap_core(value):
    return lax.ppermute(value, "c", [(0, 1), (1, 0)])


def place(slot, z0, y0):
    group, k, part = slot >> 3, (slot >> 1) & 3, slot & 1
    z = z0 ^ group ^ (group >> 1) ^ (4 * (1 - part))
    return (z << 2) | ((y0 + k) & 3)


def tokens_of(row, z0, y0):
    return place(row >> 4, z0, y0) * ROWS + (row & 15)


def project_kernel(*refs):
    count = len(refs) - 6
    pieces = refs[:count]
    wq, wkv, own, send, x, sems = refs[count:]
    copies = [
        pltpu.make_async_copy(piece, x.at[2 * i : 2 * i + 2], sems.at[i])
        for i, piece in enumerate(pieces)
    ]
    for copy in copies:
        copy.start()
    for copy in copies:
        copy.wait()
    rows = x[...].reshape(2 * ROWS * count, x.shape[2])
    kv = lax.dot_general(rows, wkv[...], (((1,), (1,)), ((), ())), preferred_element_type=F32)
    own[:, HD:] = kv
    send[:, HD:] = kv.astype(BF)
    q = jnp.dot(rows, wq[...], preferred_element_type=F32)
    own[:, :HD] = q[:, :HD]
    send[:, :HD] = q[:, HD:].astype(BF)


def join_kernel(first, second, *rest):
    pair = rest[-1]
    pair[0] = first[0]
    pair[1] = second[0]


def turn(v, cosine, sine):
    return v * cosine + pltpu.roll(v, HD // 2, 1) * sine


def kv_kernel(
    where, owner, own1, got1, own2, got2, cosine, sine, keys, values, blocks, held
):
    z0, y0, c0 = where[0], where[1], where[2]
    raw = jnp.concatenate([o[:, HD:] + g[:, HD:].astype(F32) for o, g in ((own1, got1), (own2, got2))])
    raw = raw.astype(BF)
    k = turn(raw[:, :HD].astype(F32), cosine[...], sine[...]).astype(BF)
    v = raw[:, HD:]
    keys[...] = k
    values[...] = v
    for slot in range(32):
        to = pl.multiple_of(place(slot, z0, y0) * ROWS, ROWS)
        span = slice(slot * ROWS, (slot + 1) * ROWS)
        held[pl.ds(to, ROWS), :HD] = k[span].astype(F32)
        held[pl.ds(to, ROWS), HD:] = v[span].astype(F32)
    first = y0 * 2 + c0 - owner[z0] + 64
    for z in range(NZ):
        block = (first + z * 8) & 63
        blocks[z] = held[pl.ds(pl.multiple_of(block * 8, 8), 8), :].astype(BF)


def attend_kernel(
    where, own1, got1, own2, got2, cosine, sine, keys, values, resident, out
):
    z0, y0 = where[0], where[1]
    q = jnp.concatenate([o[:, :HD] + g[:, :HD].astype(F32) for o, g in ((own1, got1), (own2, got2))])
    q = (turn(q, cosine[...], sine[...]) * HD ** (-0.5)).astype(BF)
    nt = (((1,), (1,)), ((), ()))
    old = lax.dot_general(q, resident[:, :HD], nt, preferred_element_type=F32)
    new = lax.dot_general(q, keys[...], nt, preferred_element_type=F32)
    token_q = tokens_of(lax.broadcasted_iota(jnp.int32, (TOKENS, 1), 0), z0, y0)
    token_k = tokens_of(lax.broadcasted_iota(jnp.int32, (1, TOKENS), 1), z0, y0)
    new = jnp.where(token_k <= token_q, new, masked_score)
    top = jnp.maximum(
        jnp.max(old, axis=1, keepdims=True), jnp.max(new, axis=1, keepdims=True)
    )
    old = jnp.exp(old - top)
    new = jnp.exp(new - top)
    total = jnp.sum(old, axis=1, keepdims=True) + jnp.sum(new, axis=1, keepdims=True)
    scale = 1.0 / total
    att = jnp.dot((old * scale).astype(BF), resident[:, HD:], preferred_element_type=F32)
    att = att + jnp.dot((new * scale).astype(BF), values[...], preferred_element_type=F32)
    att = att.astype(BF)
    for slot in range(32):
        to = pl.multiple_of(place(slot, z0, y0) * ROWS, ROWS)
        out[pl.ds(to, ROWS), :] = att[slot * ROWS : (slot + 1) * ROWS]


def kv_weight_kernel(where, gain, mine, one, two, three, out):
    y0 = where[1]
    for k, ref in enumerate((mine, one, two, three)):
        to = pl.multiple_of(((y0 + k) & 3) * 64, 64)
        out[pl.ds(to, 64), :] = (ref[...].astype(F32) * gain[...]).astype(BF)


VMEM = pl.BlockSpec(memory_space=pltpu.VMEM)
SMEM = pl.BlockSpec(memory_space=pltpu.SMEM)
ANY = pl.BlockSpec(memory_space=pl.ANY)


def call(kernel, shapes, specs, scratch=(), flops=0, moved=0, exps=0, limit=24):
    return pl.pallas_call(
        kernel,
        out_shape=shapes,
        in_specs=specs,
        out_specs=jax.tree.map(lambda _: VMEM, shapes),
        scratch_shapes=scratch,
        compiler_params=pltpu.CompilerParams(vmem_limit_bytes=limit * 2**20),
        cost_estimate=pl.CostEstimate(flops=flops, bytes_accessed=moved, transcendentals=exps),
    )


def shaped(*shape, dtype=BF):
    return jax.ShapeDtypeStruct(shape, dtype)


def body(residual, norm_gain, query_weight, kv_weight, resident_cache, block_start, decode_owner):
    z0, y0, c0 = (lax.axis_index(a).astype(jnp.int32) for a in ("z", "y", "c"))
    width = residual.shape[2]
    half = width // 2
    where = jnp.stack([z0, y0, c0])

    widened = residual[0].astype(F32)
    scale_row = lax.rsqrt(jnp.mean(widened * widened, axis=-1, keepdims=True) + norm_eps)
    rows = (widened * scale_row).astype(BF)
    kept = lax.dynamic_slice_in_dim(rows, c0 * half, half, 1)
    crossed = lax.dynamic_slice_in_dim(rows, (1 - c0) * half, half, 1)
    sections = lax.axis_size("s")
    steps = [
        [
            ((s * NZ + z) * 2 + c, ((s + 1) % sections * NZ + (z ^ 4)) * 2 + (c ^ flip))
            for s in range(sections)
            for z in range(NZ)
            for c in (0, 1)
        ]
        for flip in (0, 1)
    ]
    same = lax.ppermute(kept, ("s", "z", "c"), steps[0])
    other = lax.ppermute(crossed, ("s", "z", "c"), steps[1])
    piece = jnp.where(c0 == 0, jnp.stack([same, other]), jnp.stack([other, same]))
    piece = piece.reshape(1, ROWS, half)

    gain = lax.dynamic_slice_in_dim(norm_gain[0], c0 * half, half, 0)
    wq_mine = lax.dynamic_slice_in_dim(query_weight[0], c0 * half, half, 0)
    wq_given = lax.dynamic_slice_in_dim(query_weight[0], (1 - c0) * half, half, 0)
    wq_got = swap_core(wq_given)
    wq = jnp.concatenate([wq_mine, wq_got], axis=1)
    wq = (wq.astype(F32) * gain[:, None]).astype(BF)
    wkv_t = kv_weight[0].T
    kv_mine = lax.dynamic_slice_in_dim(wkv_t, c0 * half, half, 1)
    kv_given = lax.dynamic_slice_in_dim(wkv_t, (1 - c0) * half, half, 1)
    kv_got = swap_core(kv_given)
    kv_chip = jnp.where(
        c0 == 0, jnp.concatenate([kv_mine, kv_got]), jnp.concatenate([kv_got, kv_mine])
    )
    kv_others = [along_y(kv_chip, k) for k in (1, 2, 3)]
    wkv = call(kv_weight_kernel, shaped(256, half), [SMEM] + [VMEM] * 5, moved=2**22)(
        where, gain[None], kv_chip, *kv_others
    )

    tokens = tokens_of(jnp.arange(TOKENS, dtype=jnp.int32), z0, y0)
    angles = (block_start[0] + tokens).astype(F32)[:, None] * frequencies(HD)[None, :]
    cosine, sine = jnp.cos(angles), jnp.sin(angles)
    cosine = jnp.concatenate([cosine, cosine], axis=1)
    sine = jnp.concatenate([-sine, sine], axis=1)

    pair = call(join_kernel, shaped(2, ROWS, half), [VMEM] * 2 + [ANY] * 4, moved=2**19)(
        piece, across_z(piece, 4), wq, wkv, cosine, sine
    )
    groups = [pair] + [across_z(pair, k) for k in (1, 3, 2)]
    pieces = [p if k == 0 else along_y(p, k) for p in groups for k in range(NY)]

    def project(pieces):
        tokens = len(pieces) * 2 * ROWS
        return call(
            project_kernel,
            (shaped(tokens, 3 * HD, dtype=F32), shaped(tokens, 3 * HD)),
            [ANY] * len(pieces) + [VMEM] * 2,
            scratch=[
                pltpu.VMEM((2 * len(pieces), ROWS, half), BF),
                pltpu.SemaphoreType.DMA((len(pieces),)),
            ],
            flops=2 * tokens * half * 512,
            moved=9 * 2**20,
        )(*pieces, wq, wkv)

    own1, send1 = project(pieces[:12])
    got1 = swap_core(send1)
    own2, send2 = project(pieces[12:])
    got2 = swap_core(send2)
    keys, values, blocks = call(
        kv_kernel,
        (shaped(TOKENS, HD), shaped(TOKENS, HD), shaped(NZ, 8, 2 * HD)),
        [SMEM, SMEM] + [VMEM] * 6,
        scratch=[pltpu.VMEM((TOKENS, 2 * HD), F32)],
        moved=2**21,
    )(where, decode_owner[0], own1, got1, own2, got2, cosine, sine)
    spread = lax.all_to_all(blocks, "z", 0, 0)
    decode_kv = jnp.transpose(spread, (1, 0, 2))[None]
    resident = lax.dynamic_index_in_dim(resident_cache[0], z0, 0, keepdims=False)
    attn = call(
        attend_kernel,
        shaped(TOKENS, HD),
        [SMEM] + [VMEM] * 9,
        flops=4 * TOKENS * 1024 * HD,
        moved=2**21,
        exps=TOKENS * 1024,
    )(where, own1, got1, own2, got2, cosine, sine, keys, values, resident)
    return attn[None], decode_kv


def solution(mesh):
    sections = mesh.shape["section"]
    fine = Mesh(mesh.devices.reshape(sections, NZ, NY, 2), ("s", "z", "y", "c"))
    tp = ("z", "y", "c")
    return jax.shard_map(
        body,
        mesh=fine,
        in_specs=(
            P("s", tp, None),
            P("s", None),
            P("s", None, tp),
            P("s", None, tp),
            P("s", None, None, None),
            P("s"),
            P("s", None),
        ),
        out_specs=(P("s", None, tp), P("s", tp, None, None)),
        check_vma=False,
    )
```

```python
import math

import jax
import jax.numpy as jnp
from jax import lax
from jax.experimental import pallas as pl
from jax.experimental.pallas import tpu as pltpu
from jax.sharding import Mesh, PartitionSpec as P

BF = jnp.bfloat16
F32 = jnp.float32
rope_base = 500000.0
norm_eps = 1e-05
masked_score = -1e30

NZ, NY = 8, 4
ROWS = 16
TOKENS = 512
HD = 128


def frequencies(head_dim):
    half_dim = head_dim // 2
    base_freqs = jnp.exp(
        jnp.arange(half_dim, dtype=F32) * (-2.0 * math.log(rope_base) / head_dim)
    )
    wavelength = 2.0 * math.pi / base_freqs
    smooth = (8192.0 / wavelength - 1.0) / 3.0
    blended = (1.0 - smooth) * base_freqs / 8.0 + smooth * base_freqs
    return jnp.where(
        wavelength < 2048.0, base_freqs, jnp.where(wavelength > 8192.0, base_freqs / 8.0, blended)
    )


def along_y(value, k):
    return lax.ppermute(value, "y", [((i + k) % NY, i) for i in range(NY)])


def across_z(value, k):
    return lax.ppermute(value, "z", [(i, i ^ k) for i in range(NZ)])


def swap_core(value):
    return lax.ppermute(value, "c", [(0, 1), (1, 0)])


def place(slot, z0, y0):
    batch, k, i = slot >> 4, (slot >> 2) & 3, slot & 3
    z = z0 ^ i ^ (4 * (1 - batch))
    return (z << 2) | ((k + y0) & 3)


def slot_of(chip, z0, y0):
    far = (chip >> 2) ^ z0
    return ((1 - (far >> 2)) << 4) | (((chip - y0) & 3) << 2) | (far & 3)


def tokens_of(row, z0, y0):
    return place(row >> 4, z0, y0) * ROWS + (row & 15)


def project_kernel(*refs):
    *pieces, wq_far, wkv_far, _, own, send, x, wq, wkv, sems = refs
    count = len(pieces)
    copies = [
        pltpu.make_async_copy(wq_far, wq, sems.at[count]),
        pltpu.make_async_copy(wkv_far, wkv, sems.at[count + 1]),
    ]
    at = 0
    for i, piece in enumerate(pieces):
        slots = piece.shape[0]
        copies.append(pltpu.make_async_copy(piece, x.at[at : at + slots], sems.at[i]))
        at += slots
    for copy in copies:
        copy.start()
    for copy in copies:
        copy.wait()
    rows = x[...].reshape(-1, x.shape[-1])
    kv = lax.dot_general(rows, wkv[...], (((1,), (1,)), ((), ())), preferred_element_type=F32)
    own[:, HD:] = kv
    send[:, HD:] = kv.astype(BF)
    q = jnp.dot(rows, wq[...], preferred_element_type=F32)
    own[:, :HD] = q[:, :HD]
    send[:, :HD] = q[:, HD:].astype(BF)


def join_kernel(one, two, three, four, passed, *rest):
    batch, kept = rest[-2:]
    for i, piece in enumerate((one, two, three, four)):
        batch[i] = piece[...]
    kept[...] = passed[...]


def turn(v, cosine, sine):
    return v * cosine + pltpu.roll(v, HD // 2, 1) * sine


def pick_kernel(where, owner, own1, own2, blocks, held):
    z0, y0 = where[0], where[1]
    rows = own1.shape[0]
    held[:rows] = own1[:, HD:]
    held[rows:] = own2[:, HD:]
    for z in range(NZ):
        for c in (0, 1):
            block = (z * 8 + y0 * 2 + c - owner[z0]) & 63
            row = slot_of(block >> 1, z0, y0) * ROWS + (block & 1) * 8
            blocks[2 * z + c] = held[pl.ds(pl.multiple_of(row, 8), 8), :]


def decode_kernel(got, cosine, sine, out):
    for g in range(NZ):
        raw = (got[2 * g] + got[2 * g + 1]).astype(BF)
        out[g, :, :HD] = turn(raw[:, :HD].astype(F32), cosine[g], sine[g]).astype(BF)
        out[g, :, HD:] = raw[:, HD:]


def attend_kernel(where, own1, got1, own2, got2, cosine, sine, resident, out):
    z0, y0 = where[0], where[1]
    halves = ((own1, got1), (own2, got2))
    raw = jnp.concatenate([o[:, HD:] + g[:, HD:].astype(F32) for o, g in halves]).astype(BF)
    keys = turn(raw[:, :HD].astype(F32), cosine[...], sine[...]).astype(BF)
    q = jnp.concatenate([o[:, :HD] + g[:, :HD].astype(F32) for o, g in halves])
    q = (turn(q, cosine[...], sine[...]) * HD ** (-0.5)).astype(BF)
    nt = (((1,), (1,)), ((), ()))
    old = lax.dot_general(q, resident[:, :HD], nt, preferred_element_type=F32)
    new = lax.dot_general(q, keys, nt, preferred_element_type=F32)
    token_q = tokens_of(lax.broadcasted_iota(jnp.int32, (TOKENS, 1), 0), z0, y0)
    token_k = tokens_of(lax.broadcasted_iota(jnp.int32, (1, TOKENS), 1), z0, y0)
    new = jnp.where(token_k <= token_q, new, masked_score)
    top = jnp.maximum(
        jnp.max(old, axis=1, keepdims=True), jnp.max(new, axis=1, keepdims=True)
    )
    old = jnp.exp(old - top)
    new = jnp.exp(new - top)
    total = jnp.sum(old, axis=1, keepdims=True) + jnp.sum(new, axis=1, keepdims=True)
    scale = 1.0 / total
    att = jnp.dot((old * scale).astype(BF), resident[:, HD:], preferred_element_type=F32)
    att = att + jnp.dot((new * scale).astype(BF), raw[:, HD:], preferred_element_type=F32)
    att = att.astype(BF)
    for slot in range(32):
        to = pl.multiple_of(place(slot, z0, y0) * ROWS, ROWS)
        out[pl.ds(to, ROWS), :] = att[slot * ROWS : (slot + 1) * ROWS]


def kv_weight_kernel(gain, given, out):
    out[...] = (given[...].astype(F32) * gain[...]).astype(BF)


VMEM = pl.BlockSpec(memory_space=pltpu.VMEM)
SMEM = pl.BlockSpec(memory_space=pltpu.SMEM)
HBM = pl.BlockSpec(memory_space=pltpu.HBM)


def call(kernel, shapes, specs, scratch=(), flops=0, moved=0, exps=0, limit=24):
    return pl.pallas_call(
        kernel,
        out_shape=shapes,
        in_specs=specs,
        out_specs=jax.tree.map(lambda _: VMEM, shapes),
        scratch_shapes=scratch,
        compiler_params=pltpu.CompilerParams(vmem_limit_bytes=limit * 2**20),
        cost_estimate=pl.CostEstimate(flops=flops, bytes_accessed=moved, transcendentals=exps),
    )


def shaped(*shape, dtype=BF):
    return jax.ShapeDtypeStruct(shape, dtype)


def body(residual, norm_gain, query_weight, kv_weight, resident_cache, block_start, decode_owner):
    z0, y0, c0 = (lax.axis_index(a).astype(jnp.int32) for a in ("z", "y", "c"))
    width = residual.shape[2]
    half = width // 2
    where = jnp.stack([z0, y0, c0])

    widened = residual[0].astype(F32)
    scale_row = lax.rsqrt(jnp.mean(widened * widened, axis=-1, keepdims=True) + norm_eps)
    rows = (widened * scale_row).astype(BF)
    kept = lax.dynamic_slice_in_dim(rows, c0 * half, half, 1)
    crossed = lax.dynamic_slice_in_dim(rows, (1 - c0) * half, half, 1)
    sections = lax.axis_size("s")
    steps = [
        [
            ((s * NZ + z) * 2 + c, ((s + 1) % sections * NZ + (z ^ 4)) * 2 + (c ^ flip))
            for s in range(sections)
            for z in range(NZ)
            for c in (0, 1)
        ]
        for flip in (0, 1)
    ]
    same = lax.ppermute(kept, ("s", "z", "c"), steps[0])
    other = lax.ppermute(crossed, ("s", "z", "c"), steps[1])
    piece = jnp.where(c0 == 0, jnp.stack([same, other]), jnp.stack([other, same]))
    piece = piece.reshape(ROWS, half)

    gain = lax.dynamic_slice_in_dim(norm_gain[0], c0 * half, half, 0)
    wq = jnp.concatenate(
        [
            lax.dynamic_slice_in_dim(w, c0 * half, half, 0)
            for w in (query_weight[0], swap_core(query_weight[0]))
        ],
        axis=1,
    )
    wq = (wq.astype(F32) * gain[:, None]).astype(BF)
    kv_halves = jnp.transpose(kv_weight[0].T.reshape(32, 2, half), (1, 0, 2))
    kv_halves = jnp.broadcast_to(kv_halves, (NY, 2, 32, half)).reshape(NY * 2, 32, half)
    wkv = lax.all_to_all(kv_halves, ("y", "c"), 0, 0).reshape(256, half)
    wkv = call(kv_weight_kernel, shaped(256, half), [VMEM] * 2, moved=2**22)(gain[None], wkv)

    def join(one, passed, *after):
        pieces = [one] + [across_z(one, k) for k in (1, 2, 3)]
        return call(
            join_kernel,
            (shaped(4, ROWS, half), shaped(*passed.shape)),
            [VMEM] * 5 + [HBM] * len(after),
            moved=2**20,
            limit=4,
        )(*pieces, passed, *after)

    def everywhere(batch):
        return [batch] + [along_y(batch, k) for k in (1, 2, 3)]

    batch1, second = join(piece, across_z(piece, 4))
    late = (second[0, 0] > 3e38).astype(jnp.int32)

    def tables(tokens):
        angles = (block_start[0] + late + tokens).astype(F32)[..., None] * frequencies(HD)
        cosine, sine = jnp.cos(angles), jnp.sin(angles)
        return jnp.concatenate([cosine, cosine], -1), jnp.concatenate([-sine, sine], -1)

    blocks = (z0 * 8 + y0 * 2 + c0 - decode_owner[0]) & 63
    decode_tokens = (blocks * 8)[:, None] + jnp.arange(8, dtype=jnp.int32)
    row_tokens = tokens_of(jnp.arange(TOKENS, dtype=jnp.int32), z0, y0)
    cosine, sine = tables(row_tokens)
    decode_cosine, decode_sine = tables(decode_tokens)

    batch2, _ = join(second, jnp.zeros((16, HD), BF), wkv, wq, cosine, sine, decode_cosine, decode_sine)
    batch1, batch2 = everywhere(batch1), everywhere(batch2)

    def project(pieces, earlier, weight):
        slots = sum(p.shape[0] for p in pieces)
        tokens = slots * ROWS
        return call(
            project_kernel,
            (shaped(tokens, 3 * HD, dtype=F32), shaped(tokens, 3 * HD)),
            [HBM] * (len(pieces) + 3),
            scratch=[
                pltpu.VMEM((slots, ROWS, half), BF),
                pltpu.VMEM((half, 2 * HD), BF),
                pltpu.VMEM((2 * HD, half), BF),
                pltpu.SemaphoreType.DMA((len(pieces) + 2,)),
            ],
            flops=2 * tokens * half * 512 * weight,
            moved=9 * 2**20,
        )(*pieces, wq, wkv, earlier)

    own1, send1 = project(batch1, wkv, 100)
    got1 = swap_core(send1)
    own2, send2 = project(batch2, got1, 1)
    got2 = swap_core(send2)
    blocks = call(
        pick_kernel,
        shaped(NZ * 2, 8, 2 * HD, dtype=F32),
        [SMEM, SMEM] + [VMEM] * 2,
        scratch=[pltpu.VMEM((TOKENS, 2 * HD), F32)],
        moved=2**20,
        limit=4,
    )(where, decode_owner[0], own1, own2)
    blocks = lax.all_to_all(blocks, ("z", "c"), 0, 0)
    decode_kv = call(decode_kernel, shaped(NZ, 8, 2 * HD), [VMEM] * 3, moved=2**18, limit=4)(
        blocks, decode_cosine, decode_sine
    )
    decode_kv = jnp.transpose(decode_kv, (1, 0, 2))[None]
    resident = lax.dynamic_index_in_dim(resident_cache[0], z0, 0, keepdims=False)
    attn = call(
        attend_kernel,
        shaped(TOKENS, HD),
        [SMEM] + [VMEM] * 7,
        flops=4 * TOKENS * 1024 * HD,
        moved=2**21,
        exps=TOKENS * 1024,
    )(where, own1, got1, own2, got2, cosine, sine, resident)
    return attn[None], decode_kv


def solution(mesh):
    sections = mesh.shape["section"]
    fine = Mesh(mesh.devices.reshape(sections, NZ, NY, 2), ("s", "z", "y", "c"))
    tp = ("z", "y", "c")
    return jax.shard_map(
        body,
        mesh=fine,
        in_specs=(
            P("s", tp, None),
            P("s", None),
            P("s", None, tp),
            P("s", None, tp),
            P("s", None, None, None),
            P("s"),
            P("s", None),
        ),
        out_specs=(P("s", None, tp), P("s", tp, None, None)),
        check_vma=False,
    )
```

```python
import math

import jax
import jax.numpy as jnp
from jax import lax
from jax.experimental import pallas as pl
from jax.experimental.pallas import tpu as pltpu
from jax.sharding import Mesh, PartitionSpec as P

BF = jnp.bfloat16
F32 = jnp.float32
rope_base = 500000.0
norm_eps = 1e-05
masked_score = -1e30

NZ, NY = 8, 4
ROWS = 16
TOKENS = 512
HD = 128


def frequencies(head_dim):
    half_dim = head_dim // 2
    base_freqs = jnp.exp(
        jnp.arange(half_dim, dtype=F32) * (-2.0 * math.log(rope_base) / head_dim)
    )
    wavelength = 2.0 * math.pi / base_freqs
    smooth = (8192.0 / wavelength - 1.0) / 3.0
    blended = (1.0 - smooth) * base_freqs / 8.0 + smooth * base_freqs
    return jnp.where(
        wavelength < 2048.0, base_freqs, jnp.where(wavelength > 8192.0, base_freqs / 8.0, blended)
    )


def along_y(value, k):
    return lax.ppermute(value, "y", [((i + k) % NY, i) for i in range(NY)])


def across_z(value, k):
    return lax.ppermute(value, "z", [(i, i ^ k) for i in range(NZ)])


def swap_core(value):
    return lax.ppermute(value, "c", [(0, 1), (1, 0)])


def place(slot, z0, y0):
    batch, k, i = slot >> 4, (slot >> 2) & 3, slot & 3
    z = z0 ^ (batch << 1) ^ (i >> 1) ^ (4 * (1 - (i & 1)))
    return (z << 2) | ((k + y0) & 3)


def slot_of(chip, z0, y0):
    far = (chip >> 2) ^ z0
    i = ((far & 1) << 1) | (1 - (far >> 2))
    return (((far >> 1) & 1) << 4) | (((chip - y0) & 3) << 2) | i


def tokens_of(row, z0, y0):
    return place(row >> 4, z0, y0) * ROWS + (row & 15)


def project_kernel(where, *refs):
    *pieces, wq_mine, wq_other, wkv_far, _, own, send, x, wq, wkv, sems = refs
    count = len(pieces)
    half = x.shape[-1]
    rows = pl.ds(pl.multiple_of(where[2] * half, half), half)
    copies = [
        pltpu.make_async_copy(wq_mine.at[rows], wq.at[:, :HD], sems.at[count]),
        pltpu.make_async_copy(wq_other.at[rows], wq.at[:, HD:], sems.at[count + 1]),
        pltpu.make_async_copy(wkv_far, wkv, sems.at[count + 2]),
    ]
    at = 0
    for i, piece in enumerate(pieces):
        slots = piece.shape[0]
        copies.append(pltpu.make_async_copy(piece, x.at[at : at + slots], sems.at[i]))
        at += slots
    for copy in copies:
        copy.start()
    for copy in copies:
        copy.wait()
    rows = x[...].reshape(-1, x.shape[-1])
    kv = lax.dot_general(rows, wkv[...], (((1,), (1,)), ((), ())), preferred_element_type=F32)
    own[:, HD:] = kv
    send[:, HD:] = kv.astype(BF)
    q = jnp.dot(rows, wq[...], preferred_element_type=F32)
    own[:, :HD] = q[:, :HD]
    send[:, :HD] = q[:, HD:].astype(BF)


def join_kernel(one, two, *rest):
    batch = rest[-1]
    batch[:2] = one[...]
    batch[2:] = two[...]


def turn(v, cosine, sine):
    return v * cosine + pltpu.roll(v, HD // 2, 1) * sine


def pick_kernel(where, owner, own1, own2, blocks, held):
    z0, y0 = where[0], where[1]
    rows = own1.shape[0]
    held[:rows] = own1[:, HD:]
    held[rows:] = own2[:, HD:]
    for z in range(NZ):
        for c in (0, 1):
            block = (z * 8 + y0 * 2 + c - owner[z0]) & 63
            row = slot_of(block >> 1, z0, y0) * ROWS + (block & 1) * 8
            blocks[2 * z + c] = held[pl.ds(pl.multiple_of(row, 8), 8), :]


def decode_kernel(got, cosine, sine, out):
    for g in range(NZ):
        raw = (got[2 * g] + got[2 * g + 1]).astype(BF)
        out[g, :, :HD] = turn(raw[:, :HD].astype(F32), cosine[g], sine[g]).astype(BF)
        out[g, :, HD:] = raw[:, HD:]


def attend_kernel(where, own1, got1, own2, got2, cosine, sine, resident, out):
    z0, y0 = where[0], where[1]
    halves = ((own1, got1), (own2, got2))
    raw = jnp.concatenate([o[:, HD:] + g[:, HD:].astype(F32) for o, g in halves]).astype(BF)
    keys = turn(raw[:, :HD].astype(F32), cosine[...], sine[...]).astype(BF)
    q = jnp.concatenate([o[:, :HD] + g[:, :HD].astype(F32) for o, g in halves])
    q = (turn(q, cosine[...], sine[...]) * HD ** (-0.5)).astype(BF)
    nt = (((1,), (1,)), ((), ()))
    old = lax.dot_general(q, resident[:, :HD], nt, preferred_element_type=F32)
    new = lax.dot_general(q, keys, nt, preferred_element_type=F32)
    token_q = tokens_of(lax.broadcasted_iota(jnp.int32, (TOKENS, 1), 0), z0, y0)
    token_k = tokens_of(lax.broadcasted_iota(jnp.int32, (1, TOKENS), 1), z0, y0)
    new = jnp.where(token_k <= token_q, new, masked_score)
    top = jnp.maximum(
        jnp.max(old, axis=1, keepdims=True), jnp.max(new, axis=1, keepdims=True)
    )
    old = jnp.exp(old - top)
    new = jnp.exp(new - top)
    total = jnp.sum(old, axis=1, keepdims=True) + jnp.sum(new, axis=1, keepdims=True)
    scale = 1.0 / total
    att = jnp.dot((old * scale).astype(BF), resident[:, HD:], preferred_element_type=F32)
    att = att + jnp.dot((new * scale).astype(BF), raw[:, HD:], preferred_element_type=F32)
    att = att.astype(BF)
    for slot in range(32):
        to = pl.multiple_of(place(slot, z0, y0) * ROWS, ROWS)
        out[pl.ds(to, ROWS), :] = att[slot * ROWS : (slot + 1) * ROWS]


VMEM = pl.BlockSpec(memory_space=pltpu.VMEM)
SMEM = pl.BlockSpec(memory_space=pltpu.SMEM)
HBM = pl.BlockSpec(memory_space=pltpu.HBM)


def call(kernel, shapes, specs, scratch=(), flops=0, moved=0, exps=0, limit=24):
    return pl.pallas_call(
        kernel,
        out_shape=shapes,
        in_specs=specs,
        out_specs=jax.tree.map(lambda _: VMEM, shapes),
        scratch_shapes=scratch,
        compiler_params=pltpu.CompilerParams(vmem_limit_bytes=limit * 2**20),
        cost_estimate=pl.CostEstimate(flops=flops, bytes_accessed=moved, transcendentals=exps),
    )


def shaped(*shape, dtype=BF):
    return jax.ShapeDtypeStruct(shape, dtype)


def body(residual, norm_gain, query_weight, kv_weight, resident_cache, block_start, decode_owner):
    z0, y0, c0 = (lax.axis_index(a).astype(jnp.int32) for a in ("z", "y", "c"))
    width = residual.shape[2]
    half = width // 2
    where = jnp.stack([z0, y0, c0])

    widened = residual[0].astype(F32)
    scale_row = lax.rsqrt(jnp.mean(widened * widened, axis=-1, keepdims=True) + norm_eps)
    rows = (widened * scale_row).astype(BF)
    kept = lax.dynamic_slice_in_dim(rows, c0 * half, half, 1)
    crossed = lax.dynamic_slice_in_dim(rows, (1 - c0) * half, half, 1)
    sections = lax.axis_size("s")
    steps = [
        [
            ((s * NZ + z) * 2 + c, ((s + 1) % sections * NZ + (z ^ 4)) * 2 + (c ^ flip))
            for s in range(sections)
            for z in range(NZ)
            for c in (0, 1)
        ]
        for flip in (0, 1)
    ]
    same = lax.ppermute(kept, ("s", "z", "c"), steps[0])
    other = lax.ppermute(crossed, ("s", "z", "c"), steps[1])
    piece = jnp.where(c0 == 0, jnp.stack([same, other]), jnp.stack([other, same]))
    gain = lax.dynamic_slice_in_dim(norm_gain[0], c0 * half, half, 0)
    piece = (piece.reshape(ROWS, half).astype(F32) * gain[None]).astype(BF)

    wq_other = swap_core(query_weight[0])
    kv_halves = jnp.transpose(kv_weight[0].T.reshape(32, 2, half), (1, 0, 2))
    kv_halves = jnp.broadcast_to(kv_halves, (NY, 2, 32, half)).reshape(NY * 2, 32, half)
    wkv = lax.all_to_all(kv_halves, ("y", "c"), 0, 0).reshape(256, half)

    pair = jnp.stack([piece, across_z(piece, 4)])

    def join(one, two, *after):
        return call(
            join_kernel,
            shaped(4, ROWS, half),
            [VMEM] * 2 + [HBM] * len(after),
            moved=2**20,
            limit=4,
        )(one, two, *after)

    batch1 = join(pair, across_z(pair, 1), wq_other)
    late = (batch1[0, 0, 0] > 3e38).astype(jnp.int32)

    def tables(tokens):
        angles = (block_start[0] + late + tokens).astype(F32)[..., None] * frequencies(HD)
        cosine, sine = jnp.cos(angles), jnp.sin(angles)
        return jnp.concatenate([cosine, cosine], -1), jnp.concatenate([-sine, sine], -1)

    blocks = (z0 * 8 + y0 * 2 + c0 - decode_owner[0]) & 63
    decode_tokens = (blocks * 8)[:, None] + jnp.arange(8, dtype=jnp.int32)
    row_tokens = tokens_of(jnp.arange(TOKENS, dtype=jnp.int32), z0, y0)
    cosine, sine = tables(row_tokens)
    decode_cosine, decode_sine = tables(decode_tokens)

    made = (wkv, cosine, sine, decode_cosine, decode_sine)
    batch2 = join(across_z(pair, 2), across_z(pair, 3), *made)
    batch1, batch2 = (
        [batch] + [along_y(batch, k) for k in (1, 2, 3)] for batch in (batch1, batch2)
    )

    def project(pieces, earlier, weight):
        slots = sum(p.shape[0] for p in pieces)
        tokens = slots * ROWS
        return call(
            project_kernel,
            (shaped(tokens, 3 * HD, dtype=F32), shaped(tokens, 3 * HD)),
            [SMEM] + [HBM] * (len(pieces) + 4),
            scratch=[
                pltpu.VMEM((slots, ROWS, half), BF),
                pltpu.VMEM((half, 2 * HD), BF),
                pltpu.VMEM((2 * HD, half), BF),
                pltpu.SemaphoreType.DMA((len(pieces) + 3,)),
            ],
            flops=2 * tokens * half * 512 * weight,
            moved=9 * 2**20,
        )(where, *pieces, query_weight[0], wq_other, wkv, earlier)

    own1, send1 = project(batch1, wkv, 100)
    got1 = swap_core(send1)
    own2, send2 = project(batch2, got1, 1)
    got2 = swap_core(send2)
    blocks = call(
        pick_kernel,
        shaped(NZ * 2, 8, 2 * HD, dtype=F32),
        [SMEM, SMEM] + [VMEM] * 2,
        scratch=[pltpu.VMEM((TOKENS, 2 * HD), F32)],
        moved=2**20,
        limit=4,
    )(where, decode_owner[0], own1, own2)
    blocks = lax.all_to_all(blocks, ("z", "c"), 0, 0)
    decode_kv = call(decode_kernel, shaped(NZ, 8, 2 * HD), [VMEM] * 3, moved=2**18, limit=4)(
        blocks, decode_cosine, decode_sine
    )
    decode_kv = jnp.transpose(decode_kv, (1, 0, 2))[None]
    resident = lax.dynamic_index_in_dim(resident_cache[0], z0, 0, keepdims=False)
    attn = call(
        attend_kernel,
        shaped(TOKENS, HD),
        [SMEM] + [VMEM] * 7,
        flops=4 * TOKENS * 1024 * HD,
        moved=2**21,
        exps=TOKENS * 1024,
    )(where, own1, got1, own2, got2, cosine, sine, resident)
    return attn[None], decode_kv


def solution(mesh):
    sections = mesh.shape["section"]
    fine = Mesh(mesh.devices.reshape(sections, NZ, NY, 2), ("s", "z", "y", "c"))
    tp = ("z", "y", "c")
    return jax.shard_map(
        body,
        mesh=fine,
        in_specs=(
            P("s", tp, None),
            P("s", None),
            P("s", None, tp),
            P("s", None, tp),
            P("s", None, None, None),
            P("s"),
            P("s", None),
        ),
        out_specs=(P("s", None, tp), P("s", tp, None, None)),
        check_vma=False,
    )
```

```python
import math

import jax
import jax.numpy as jnp
from jax import lax
from jax.experimental import pallas as pl
from jax.experimental.pallas import tpu as pltpu
from jax.sharding import Mesh, PartitionSpec as P

BF = jnp.bfloat16
F32 = jnp.float32
rope_base = 500000.0
norm_eps = 1e-05
masked_score = -1e30

NZ, NY = 8, 4
ROWS = 16
TOKENS = 512
HD = 128


def frequencies(head_dim):
    half_dim = head_dim // 2
    base_freqs = jnp.exp(
        jnp.arange(half_dim, dtype=F32) * (-2.0 * math.log(rope_base) / head_dim)
    )
    wavelength = 2.0 * math.pi / base_freqs
    smooth = (8192.0 / wavelength - 1.0) / 3.0
    blended = (1.0 - smooth) * base_freqs / 8.0 + smooth * base_freqs
    return jnp.where(
        wavelength < 2048.0, base_freqs, jnp.where(wavelength > 8192.0, base_freqs / 8.0, blended)
    )


def along_y(value, k):
    return lax.ppermute(value, "y", [((i + k) % NY, i) for i in range(NY)])


def across_z(value, k):
    return lax.ppermute(value, "z", [(i, i ^ k) for i in range(NZ)])


def swap_core(value):
    return lax.ppermute(value, "c", [(0, 1), (1, 0)])


def place(slot, z0, y0):
    inner = (slot >= 8) & (slot < 24)
    k = jnp.where(inner, (slot - 8) >> 2, (slot >> 1) & 3)
    step = jnp.where(inner, 1 + (slot & 2), jnp.where(slot < 8, 0, 2))
    z = z0 ^ step ^ (4 * (1 - (slot & 1)))
    return (z << 2) | ((k + y0) & 3)


def slot_of(chip, z0, y0):
    far = (chip >> 2) ^ z0
    step, part, k = far & 3, 1 - (far >> 2), (chip - y0) & 3
    outer = jnp.where(step == 0, 0, 24) + 2 * k + part
    return jnp.where((step & 1) == 1, 8 + 4 * k + (step & 2) + part, outer)


def tokens_of(row, z0, y0):
    return place(row >> 4, z0, y0) * ROWS + (row & 15)


def project(pieces, copies, wq, wkv, own, send, x, sems):
    copies += [
        pltpu.make_async_copy(piece, x.at[at : at + piece.shape[0]], sems.at[i])
        for i, (piece, at) in enumerate(pieces)
    ]
    for copy in copies:
        copy.start()
    for copy in copies:
        copy.wait()
    rows = x[...].reshape(-1, x.shape[-1])
    kv = lax.dot_general(rows, wkv[...], (((1,), (1,)), ((), ())), preferred_element_type=F32)
    own[:, HD:] = kv
    send[:, HD:] = kv.astype(BF)
    q = jnp.dot(rows, wq[...], preferred_element_type=F32)
    own[:, :HD] = q[:, :HD]
    send[:, :HD] = q[:, HD:].astype(BF)


def first_kernel(where, *refs):
    *pieces, wq_mine, wq_other, wkv_far, own, send, wq, x, wkv, sems = refs
    half = x.shape[-1]
    rows = pl.ds(pl.multiple_of(where[2] * half, half), half)
    copies = [
        pltpu.make_async_copy(wq_mine.at[rows], wq.at[:, :HD], sems.at[8]),
        pltpu.make_async_copy(wq_other.at[rows], wq.at[:, HD:], sems.at[9]),
        pltpu.make_async_copy(wkv_far, wkv, sems.at[10]),
    ]
    places = [2 * k for k in range(NY)] + [8 + 4 * k for k in range(NY)]
    project(list(zip(pieces, places)), copies, wq, wkv, own, send, x, sems)


def second_kernel(*refs):
    pieces, (wq, wkv), (own, send, x, sems) = refs[:NY], refs[NY : NY + 2], refs[-4:]
    places = [2 * k for k in range(NY)]
    project(list(zip(pieces, places)), [], wq, wkv, own, send, x, sems)


def join_kernel(one, two, *rest):
    batch = rest[-1]
    count = one.shape[0]
    batch[:count] = one[...]
    batch[count:] = two[...]


def turn(v, cosine, sine):
    return v * cosine + pltpu.roll(v, HD // 2, 1) * sine


def pick_kernel(where, owner, own1, own2, blocks, held):
    z0, y0 = where[0], where[1]
    rows = own1.shape[0]
    held[:rows] = own1[:, HD:]
    held[rows:] = own2[:, HD:]
    for z in range(NZ):
        for c in (0, 1):
            block = (z * 8 + y0 * 2 + c - owner[z0]) & 63
            row = slot_of(block >> 1, z0, y0) * ROWS + (block & 1) * 8
            blocks[2 * z + c] = held[pl.ds(pl.multiple_of(row, 8), 8), :]


def decode_kernel(got, tables, out):
    heads = []
    for g in range(NZ):
        raw = (got[2 * g] + got[2 * g + 1]).astype(BF).astype(F32)
        k = turn(raw[:, :HD], tables[g, :, :HD], tables[g, :, HD:])
        heads.append(jnp.concatenate([k, raw[:, HD:]], axis=1))
    out[...] = jnp.stack(heads, axis=1).astype(BF)


def attend_kernel(where, own1, got1, own2, got2, cosine, sine, resident, out):
    z0, y0 = where[0], where[1]
    halves = ((own1, got1), (own2, got2))
    raw = jnp.concatenate([o[:, HD:] + g[:, HD:].astype(F32) for o, g in halves]).astype(BF)
    keys = turn(raw[:, :HD].astype(F32), cosine[...], sine[...]).astype(BF)
    q = jnp.concatenate([o[:, :HD] + g[:, :HD].astype(F32) for o, g in halves])
    q = (turn(q, cosine[...], sine[...]) * HD ** (-0.5)).astype(BF)
    nt = (((1,), (1,)), ((), ()))
    old = lax.dot_general(q, resident[:, :HD], nt, preferred_element_type=F32)
    new = lax.dot_general(q, keys, nt, preferred_element_type=F32)
    token_q = tokens_of(lax.broadcasted_iota(jnp.int32, (TOKENS, 1), 0), z0, y0)
    token_k = tokens_of(lax.broadcasted_iota(jnp.int32, (1, TOKENS), 1), z0, y0)
    new = jnp.where(token_k <= token_q, new, masked_score)
    top = jnp.maximum(
        jnp.max(old, axis=1, keepdims=True), jnp.max(new, axis=1, keepdims=True)
    )
    old = jnp.exp(old - top)
    new = jnp.exp(new - top)
    total = jnp.sum(old, axis=1, keepdims=True) + jnp.sum(new, axis=1, keepdims=True)
    scale = 1.0 / total
    att = jnp.dot((old * scale).astype(BF), resident[:, HD:], preferred_element_type=F32)
    att = att + jnp.dot((new * scale).astype(BF), raw[:, HD:], preferred_element_type=F32)
    att = att.astype(BF)
    for slot in range(32):
        to = pl.multiple_of(place(slot, z0, y0) * ROWS, ROWS)
        out[pl.ds(to, ROWS), :] = att[slot * ROWS : (slot + 1) * ROWS]


VMEM = pl.BlockSpec(memory_space=pltpu.VMEM)
SMEM = pl.BlockSpec(memory_space=pltpu.SMEM)
HBM = pl.BlockSpec(memory_space=pltpu.HBM)


def call(kernel, shapes, specs, scratch=(), flops=0, moved=0, exps=0, limit=24):
    return pl.pallas_call(
        kernel,
        out_shape=shapes,
        in_specs=specs,
        out_specs=jax.tree.map(lambda _: VMEM, shapes),
        scratch_shapes=scratch,
        compiler_params=pltpu.CompilerParams(vmem_limit_bytes=limit * 2**20),
        cost_estimate=pl.CostEstimate(flops=flops, bytes_accessed=moved, transcendentals=exps),
    )


def shaped(*shape, dtype=BF):
    return jax.ShapeDtypeStruct(shape, dtype)


def body(residual, norm_gain, query_weight, kv_weight, resident_cache, block_start, decode_owner):
    z0, y0, c0 = (lax.axis_index(a).astype(jnp.int32) for a in ("z", "y", "c"))
    width = residual.shape[2]
    half = width // 2
    where = jnp.stack([z0, y0, c0])

    widened = residual[0].astype(F32)
    scale_row = lax.rsqrt(jnp.mean(widened * widened, axis=-1, keepdims=True) + norm_eps)
    rows = (widened * scale_row).astype(BF)
    kept = lax.dynamic_slice_in_dim(rows, c0 * half, half, 1)
    crossed = lax.dynamic_slice_in_dim(rows, (1 - c0) * half, half, 1)
    sections = lax.axis_size("s")
    steps = [
        [
            ((s * NZ + z) * 2 + c, ((s + 1) % sections * NZ + (z ^ 4)) * 2 + (c ^ flip))
            for s in range(sections)
            for z in range(NZ)
            for c in (0, 1)
        ]
        for flip in (0, 1)
    ]
    same = lax.ppermute(kept, ("s", "z", "c"), steps[0])
    other = lax.ppermute(crossed, ("s", "z", "c"), steps[1])
    piece = jnp.where(c0 == 0, jnp.stack([same, other]), jnp.stack([other, same]))
    gain = lax.dynamic_slice_in_dim(norm_gain[0], c0 * half, half, 0)
    piece = (piece.reshape(ROWS, half).astype(F32) * gain[None]).astype(BF)

    wq_other = swap_core(query_weight[0])
    kv_halves = jnp.transpose(kv_weight[0].T.reshape(32, 2, half), (1, 0, 2))
    kv_halves = jnp.broadcast_to(kv_halves, (NY, 2, 32, half)).reshape(NY * 2, 32, half)
    wkv = lax.all_to_all(kv_halves, ("y", "c"), 0, 0).reshape(256, half)

    def join(one, two, *after):
        return call(
            join_kernel,
            shaped(one.shape[0] + two.shape[0], ROWS, half),
            [VMEM] * 2 + [HBM] * len(after),
            moved=2**20,
            limit=4,
        )(one, two, *after)

    def everywhere(batch):
        return [batch] + [along_y(batch, k) for k in (1, 2, 3)]

    piece = piece[None]
    second = across_z(piece, 4)
    pair = jnp.concatenate([piece, second])
    batch1 = join(across_z(pair, 1), across_z(pair, 3), wq_other, wkv)
    late = (batch1[0, 0, 0] > 3e38).astype(jnp.int32)

    def tables(tokens):
        angles = (block_start[0] + late + tokens).astype(F32)[..., None] * frequencies(HD)
        cosine, sine = jnp.cos(angles), jnp.sin(angles)
        return jnp.concatenate([cosine, cosine], -1), jnp.concatenate([-sine, sine], -1)

    blocks = (z0 * 8 + y0 * 2 + c0 - decode_owner[0]) & 63
    decode_tokens = (blocks * 8)[:, None] + jnp.arange(8, dtype=jnp.int32)
    row_tokens = tokens_of(jnp.arange(TOKENS, dtype=jnp.int32), z0, y0)
    cosine, sine = tables(row_tokens)
    decode_tables = jnp.concatenate(tables(decode_tokens), -1)

    pieces1 = everywhere(pair) + everywhere(batch1)
    pieces2 = everywhere(across_z(pair, 2))

    def projected(rows):
        return shaped(rows, 3 * HD, dtype=F32), shaped(rows, 3 * HD)

    own1, send1, wq = call(
        first_kernel,
        (*projected(384), shaped(half, 2 * HD)),
        [SMEM] + [HBM] * 11,
        scratch=[
            pltpu.VMEM((24, ROWS, half), BF),
            pltpu.VMEM((2 * HD, half), BF),
            pltpu.SemaphoreType.DMA((11,)),
        ],
        flops=200 * 384 * half * 512,
        moved=9 * 2**20,
    )(where, *pieces1, query_weight[0], wq_other, wkv)
    got1 = swap_core(send1)
    own2, send2 = call(
        second_kernel,
        projected(128),
        [HBM] * 4 + [VMEM] * 2 + [HBM] * 4,
        scratch=[pltpu.VMEM((8, ROWS, half), BF), pltpu.SemaphoreType.DMA((4,))],
        flops=2 * 128 * half * 512,
        moved=9 * 2**20,
    )(*pieces2, wq, wkv, got1, cosine, sine, decode_tables)
    got2 = swap_core(send2)
    blocks = call(
        pick_kernel,
        shaped(NZ * 2, 8, 2 * HD, dtype=F32),
        [SMEM, SMEM] + [VMEM] * 2,
        scratch=[pltpu.VMEM((TOKENS, 2 * HD), F32)],
        moved=2**20,
        limit=4,
    )(where, decode_owner[0], own1, own2)
    blocks = lax.all_to_all(blocks, ("z", "c"), 0, 0)
    decode_kv = call(decode_kernel, shaped(8, NZ, 2 * HD), [VMEM] * 2, moved=2**18, limit=4)(
        blocks, decode_tables
    )
    resident = lax.dynamic_index_in_dim(resident_cache[0], z0, 0, keepdims=False)
    attn = call(
        attend_kernel,
        shaped(TOKENS, HD),
        [SMEM] + [VMEM] * 7,
        flops=4 * TOKENS * 1024 * HD,
        moved=2**21,
        exps=TOKENS * 1024,
    )(where, own1, got1, own2, got2, cosine, sine, resident)
    return attn[None], decode_kv[None]


def solution(mesh):
    sections = mesh.shape["section"]
    fine = Mesh(mesh.devices.reshape(sections, NZ, NY, 2), ("s", "z", "y", "c"))
    tp = ("z", "y", "c")
    return jax.shard_map(
        body,
        mesh=fine,
        in_specs=(
            P("s", tp, None),
            P("s", None),
            P("s", None, tp),
            P("s", None, tp),
            P("s", None, None, None),
            P("s"),
            P("s", None),
        ),
        out_specs=(P("s", None, tp), P("s", tp, None, None)),
        check_vma=False,
    )
```

```python
import math

import jax
import jax.numpy as jnp
from jax import lax
from jax.experimental import pallas as pl
from jax.experimental.pallas import tpu as pltpu
from jax.sharding import Mesh, PartitionSpec as P

BF = jnp.bfloat16
F32 = jnp.float32
rope_base = 500000.0
norm_eps = 1e-05
masked_score = -1e30

NZ, NY = 8, 4
ROWS = 16
TOKENS = 512
HD = 128


def frequencies(head_dim):
    half_dim = head_dim // 2
    base_freqs = jnp.exp(
        jnp.arange(half_dim, dtype=F32) * (-2.0 * math.log(rope_base) / head_dim)
    )
    wavelength = 2.0 * math.pi / base_freqs
    smooth = (8192.0 / wavelength - 1.0) / 3.0
    blended = (1.0 - smooth) * base_freqs / 8.0 + smooth * base_freqs
    return jnp.where(
        wavelength < 2048.0, base_freqs, jnp.where(wavelength > 8192.0, base_freqs / 8.0, blended)
    )


def along_y(value, k):
    return lax.ppermute(value, "y", [((i + k) % NY, i) for i in range(NY)])


def across_z(value, k):
    return lax.ppermute(value, "z", [(i, i ^ k) for i in range(NZ)])


def swap_core(value):
    return lax.ppermute(value, "c", [(0, 1), (1, 0)])


def place(slot, z0, y0):
    batch, k, i = slot >> 4, (slot >> 2) & 3, slot & 3
    z = z0 ^ (batch << 1) ^ (i >> 1) ^ (4 * (1 - (i & 1)))
    return (z << 2) | ((k + y0) & 3)


def slot_of(chip, z0, y0):
    far = (chip >> 2) ^ z0
    i = ((far & 1) << 1) | (1 - (far >> 2))
    return (((far >> 1) & 1) << 4) | (((chip - y0) & 3) << 2) | i


def tokens_of(row, z0, y0):
    return place(row >> 4, z0, y0) * ROWS + (row & 15)


PLACES = (0, 4, 8, 10, 12)


def project(pieces, copies, wq, wkv, own, send, x, sems):
    copies += [
        pltpu.make_async_copy(piece, x.at[at : at + piece.shape[0]], sems.at[i])
        for i, (piece, at) in enumerate(zip(pieces, PLACES))
    ]
    for copy in copies:
        copy.start()
    for copy in copies:
        copy.wait()
    rows = x[...].reshape(-1, x.shape[-1])
    kv = lax.dot_general(rows, wkv[...], (((1,), (1,)), ((), ())), preferred_element_type=F32)
    own[:, HD:] = kv
    send[:, HD:] = kv.astype(BF)
    q = jnp.dot(rows, wq[...], preferred_element_type=F32)
    own[:, :HD] = q[:, :HD]
    send[:, :HD] = q[:, HD:].astype(BF)


def first_kernel(where, *refs):
    *pieces, wq_mine, wq_other, wkv_far, own, send, wq, wkv, x, sems = refs
    half = x.shape[-1]
    rows = pl.ds(pl.multiple_of(where[2] * half, half), half)
    copies = [
        pltpu.make_async_copy(wq_mine.at[rows], wq.at[:, :HD], sems.at[5]),
        pltpu.make_async_copy(wq_other, wq.at[:, HD:], sems.at[6]),
        pltpu.make_async_copy(wkv_far, wkv, sems.at[7]),
    ]
    project(pieces, copies, wq, wkv, own, send, x, sems)


def second_kernel(where, owner, *refs):
    pieces, (wq, wkv, first), (own, send, blocks, x, held, sems) = refs[:5], refs[5:8], refs[8:]
    project(pieces, [], wq, wkv, own, send, x, sems)
    z0, y0 = where[0], where[1]
    rows = own.shape[0]
    held[:rows] = first[:, HD:]
    held[rows:] = own[:, HD:]
    for z in range(NZ):
        for c in (0, 1):
            block = (z * 8 + y0 * 2 + c - owner[z0]) & 63
            row = slot_of(block >> 1, z0, y0) * ROWS + (block & 1) * 8
            blocks[2 * z + c] = held[pl.ds(pl.multiple_of(row, 8), 8), :]


def spread_kernel(kv, out, sems):
    half = out.shape[-1]
    copies = [
        pltpu.make_async_copy(kv.at[:, pl.ds((i & 1) * half, half)], out.at[i], sems.at[i])
        for i in range(NY * 2)
    ]
    for copy in copies:
        copy.start()
    for copy in copies:
        copy.wait()


def join_kernel(one, two, *rest):
    batch = rest[-1]
    batch[:2] = one[...]
    batch[2:] = two[...]


def turn(v, cosine, sine):
    return v * cosine + pltpu.roll(v, HD // 2, 1) * sine


def decode_kernel(got, tables, out):
    for g in range(NZ):
        raw = (got[2 * g] + got[2 * g + 1]).astype(BF)
        out[g, :, :HD] = turn(
            raw[:, :HD].astype(F32), tables[g, :, :HD], tables[g, :, HD:]
        ).astype(BF)
        out[g, :, HD:] = raw[:, HD:]


def attend_kernel(where, own1, got1, own2, got2, cosine, sine, resident, out):
    z0, y0 = where[0], where[1]
    halves = ((own1, got1), (own2, got2))
    raw = jnp.concatenate([o[:, HD:] + g[:, HD:].astype(F32) for o, g in halves]).astype(BF)
    keys = turn(raw[:, :HD].astype(F32), cosine[...], sine[...]).astype(BF)
    q = jnp.concatenate([o[:, :HD] + g[:, :HD].astype(F32) for o, g in halves])
    q = (turn(q, cosine[...], sine[...]) * HD ** (-0.5)).astype(BF)
    nt = (((1,), (1,)), ((), ()))
    old = lax.dot_general(q, resident[:, :HD], nt, preferred_element_type=F32)
    new = lax.dot_general(q, keys, nt, preferred_element_type=F32)
    token_q = tokens_of(lax.broadcasted_iota(jnp.int32, (TOKENS, 1), 0), z0, y0)
    token_k = tokens_of(lax.broadcasted_iota(jnp.int32, (1, TOKENS), 1), z0, y0)
    new = jnp.where(token_k <= token_q, new, masked_score)
    top = jnp.maximum(
        jnp.max(old, axis=1, keepdims=True), jnp.max(new, axis=1, keepdims=True)
    )
    old = jnp.exp(old - top)
    new = jnp.exp(new - top)
    total = jnp.sum(old, axis=1, keepdims=True) + jnp.sum(new, axis=1, keepdims=True)
    scale = 1.0 / total
    att = jnp.dot((old * scale).astype(BF), resident[:, HD:], preferred_element_type=F32)
    att = att + jnp.dot((new * scale).astype(BF), raw[:, HD:], preferred_element_type=F32)
    att = att.astype(BF)
    for slot in range(32):
        to = pl.multiple_of(place(slot, z0, y0) * ROWS, ROWS)
        out[pl.ds(to, ROWS), :] = att[slot * ROWS : (slot + 1) * ROWS]


VMEM = pl.BlockSpec(memory_space=pltpu.VMEM)
SMEM = pl.BlockSpec(memory_space=pltpu.SMEM)
HBM = pl.BlockSpec(memory_space=pltpu.HBM)


def call(kernel, shapes, specs, scratch=(), flops=0, moved=0, exps=0, limit=24, out=VMEM):
    return pl.pallas_call(
        kernel,
        out_shape=shapes,
        in_specs=specs,
        out_specs=jax.tree.map(lambda _: out, shapes),
        scratch_shapes=scratch,
        compiler_params=pltpu.CompilerParams(vmem_limit_bytes=limit * 2**20),
        cost_estimate=pl.CostEstimate(flops=flops, bytes_accessed=moved, transcendentals=exps),
    )


def shaped(*shape, dtype=BF):
    return jax.ShapeDtypeStruct(shape, dtype)


def body(residual, norm_gain, query_weight, kv_weight, resident_cache, block_start, decode_owner):
    z0, y0, c0 = (lax.axis_index(a).astype(jnp.int32) for a in ("z", "y", "c"))
    width = residual.shape[2]
    half = width // 2
    where = jnp.stack([z0, y0, c0])

    widened = residual[0].astype(F32)
    scale_row = lax.rsqrt(jnp.mean(widened * widened, axis=-1, keepdims=True) + norm_eps)
    rows = (widened * scale_row).astype(BF)
    kept = lax.dynamic_slice_in_dim(rows, c0 * half, half, 1)
    crossed = lax.dynamic_slice_in_dim(rows, (1 - c0) * half, half, 1)
    sections = lax.axis_size("s")
    steps = [
        [
            ((s * NZ + z) * 2 + c, ((s + 1) % sections * NZ + (z ^ 4)) * 2 + (c ^ flip))
            for s in range(sections)
            for z in range(NZ)
            for c in (0, 1)
        ]
        for flip in (0, 1)
    ]
    same = lax.ppermute(kept, ("s", "z", "c"), steps[0])
    other = lax.ppermute(crossed, ("s", "z", "c"), steps[1])
    piece = jnp.where(c0 == 0, jnp.stack([same, other]), jnp.stack([other, same]))
    gain = lax.dynamic_slice_in_dim(norm_gain[0], c0 * half, half, 0)
    piece = (piece.reshape(ROWS, half).astype(F32) * gain[None]).astype(BF)

    arrived = (piece[0, 0] > 3e38).astype(jnp.int32)
    wq_other = swap_core(
        lax.dynamic_slice_in_dim(query_weight[0], (1 - c0) * half + arrived, half, 0)
    )
    kv_halves = call(spread_kernel, shaped(NY * 2, 32, half), [HBM], moved=2**22, limit=4,
        scratch=[pltpu.SemaphoreType.DMA((NY * 2,))], out=HBM)(kv_weight[0].T)
    wkv = lax.all_to_all(kv_halves, ("y", "c"), 0, 0).reshape(256, half)

    pair = jnp.stack([piece, across_z(piece, 4)])

    def join(one, two, *after):
        return call(
            join_kernel,
            shaped(4, ROWS, half),
            [VMEM] * 2 + [HBM] * len(after),
            moved=2**20,
            limit=4,
        )(one, two, *after)

    batch1 = join(pair, across_z(pair, 1), wq_other)
    late = (batch1[0, 0, 0] > 3e38).astype(jnp.int32)

    def tables(tokens):
        angles = (block_start[0] + late + tokens).astype(F32)[..., None] * frequencies(HD)
        cosine, sine = jnp.cos(angles), jnp.sin(angles)
        return jnp.concatenate([cosine, cosine], -1), jnp.concatenate([-sine, sine], -1)

    blocks = (z0 * 8 + y0 * 2 + c0 - decode_owner[0]) & 63
    decode_tokens = (blocks * 8)[:, None] + jnp.arange(8, dtype=jnp.int32)
    row_tokens = tokens_of(jnp.arange(TOKENS, dtype=jnp.int32), z0, y0)
    cosine, sine = tables(row_tokens)
    decode_tables = jnp.concatenate(tables(decode_tokens), -1)

    batch2 = join(across_z(pair, 2), across_z(pair, 3), wkv, cosine, sine, decode_tables)

    def everywhere(batch):
        after, before = along_y(batch, 1), along_y(batch, 3)
        return [batch, after, along_y(before[:2], 3), along_y(after[2:], 1), before]

    rows = TOKENS // 2
    projected = (shaped(rows, 3 * HD, dtype=F32), shaped(rows, 3 * HD))
    scratch = pltpu.VMEM((rows // ROWS, ROWS, half), BF)
    own1, send1, *weights = call(
        first_kernel,
        (*projected, shaped(half, 2 * HD), shaped(2 * HD, half)),
        [SMEM] + [HBM] * 8,
        scratch=[scratch, pltpu.SemaphoreType.DMA((8,))],
        flops=200 * rows * half * 512,
        moved=9 * 2**20,
    )(where, *everywhere(batch1), query_weight[0], wq_other, wkv)
    got1 = swap_core(send1)
    own2, send2, blocks = call(
        second_kernel,
        (*projected, shaped(NZ * 2, 8, 2 * HD, dtype=F32)),
        [SMEM, SMEM] + [HBM] * 5 + [VMEM] * 3,
        scratch=[scratch, pltpu.VMEM((TOKENS, 2 * HD), F32), pltpu.SemaphoreType.DMA((5,))],
        flops=2 * rows * half * 512,
        moved=9 * 2**20,
    )(where, decode_owner[0], *everywhere(batch2), *weights, own1)
    got2 = swap_core(send2)
    blocks = lax.all_to_all(blocks, ("z", "c"), 0, 0)
    decode_kv = call(decode_kernel, shaped(NZ, 8, 2 * HD), [VMEM] * 2, moved=2**18, limit=4)(
        blocks, decode_tables
    )
    decode_kv = jnp.transpose(decode_kv, (1, 0, 2))[None]
    resident = lax.dynamic_index_in_dim(resident_cache[0], z0, 0, keepdims=False)
    attn = call(
        attend_kernel,
        shaped(TOKENS, HD),
        [SMEM] + [VMEM] * 7,
        flops=4 * TOKENS * 1024 * HD,
        moved=2**21,
        exps=TOKENS * 1024,
    )(where, own1, got1, own2, got2, cosine, sine, resident)
    return attn[None], decode_kv


def solution(mesh):
    sections = mesh.shape["section"]
    fine = Mesh(mesh.devices.reshape(sections, NZ, NY, 2), ("s", "z", "y", "c"))
    tp = ("z", "y", "c")
    return jax.shard_map(
        body,
        mesh=fine,
        in_specs=(
            P("s", tp, None),
            P("s", None),
            P("s", None, tp),
            P("s", None, tp),
            P("s", None, None, None),
            P("s"),
            P("s", None),
        ),
        out_specs=(P("s", None, tp), P("s", tp, None, None)),
        check_vma=False,
    )
```

```python
import math

import jax
import jax.numpy as jnp
from jax import lax
from jax.experimental import pallas as pl
from jax.experimental.pallas import tpu as pltpu
from jax.sharding import Mesh, PartitionSpec as P

BF = jnp.bfloat16
F32 = jnp.float32
rope_base = 500000.0
norm_eps = 1e-05
masked_score = -1e30

NZ, NY = 8, 4
ROWS = 16
TOKENS = 512
HD = 128


def frequencies(head_dim):
    half_dim = head_dim // 2
    base_freqs = jnp.exp(
        jnp.arange(half_dim, dtype=F32) * (-2.0 * math.log(rope_base) / head_dim)
    )
    wavelength = 2.0 * math.pi / base_freqs
    smooth = (8192.0 / wavelength - 1.0) / 3.0
    blended = (1.0 - smooth) * base_freqs / 8.0 + smooth * base_freqs
    return jnp.where(
        wavelength < 2048.0, base_freqs, jnp.where(wavelength > 8192.0, base_freqs / 8.0, blended)
    )


def along_y(value, k):
    return lax.ppermute(value, "y", [((i + k) % NY, i) for i in range(NY)])


def across_z(value, k):
    return lax.ppermute(value, "z", [(i, i ^ k) for i in range(NZ)])


def swap_core(value):
    return lax.ppermute(value, "c", [(0, 1), (1, 0)])


def place(slot, z0, y0):
    batch, k, i = slot >> 4, (slot >> 2) & 3, slot & 3
    z = z0 ^ (batch << 1) ^ (i >> 1) ^ (4 * (1 - (i & 1)))
    return (z << 2) | ((k + y0) & 3)


def slot_of(chip, z0, y0):
    far = (chip >> 2) ^ z0
    i = ((far & 1) << 1) | (1 - (far >> 2))
    return (((far >> 1) & 1) << 4) | (((chip - y0) & 3) << 2) | i


def tokens_of(row, z0, y0):
    return place(row >> 4, z0, y0) * ROWS + (row & 15)


PLACES = (0, 4, 8, 10, 12)


def project(pieces, early, late, wq, wkv, own, send, x, sems):
    early += [
        pltpu.make_async_copy(piece, x.at[at : at + piece.shape[0]], sems.at[i])
        for i, (piece, at) in enumerate(zip(pieces, PLACES))
    ]
    for copy in early + late:
        copy.start()
    for copy in early:
        copy.wait()
    rows = x[...].reshape(-1, x.shape[-1])
    kv = lax.dot_general(rows, wkv[...], (((1,), (1,)), ((), ())), preferred_element_type=F32)
    own[:, HD:] = kv
    send[:, HD:] = kv.astype(BF)
    for copy in late:
        copy.wait()
    q = jnp.dot(rows, wq[...], preferred_element_type=F32)
    own[:, :HD] = q[:, :HD]
    send[:, :HD] = q[:, HD:].astype(BF)


def first_kernel(where, *refs):
    *pieces, wq_mine, wq_other, wkv_far, own, send, wq, wkv, x, sems = refs
    half = x.shape[-1]
    rows = pl.ds(pl.multiple_of(where[2] * half, half), half)
    early = [pltpu.make_async_copy(wkv_far, wkv, sems.at[7])]
    late = [
        pltpu.make_async_copy(wq_mine.at[rows], wq.at[:, :HD], sems.at[5]),
        pltpu.make_async_copy(wq_other, wq.at[:, HD:], sems.at[6]),
    ]
    project(pieces, early, late, wq, wkv, own, send, x, sems)


def second_kernel(where, owner, *refs):
    pieces, (wq, wkv, own1, send1), (own, send, blocks, x, held, sems) = refs[:5], refs[5:9], refs[9:]
    rows = own.shape[0]
    send[:rows] = send1[...]
    project(pieces, [], [], wq, wkv, own, send.at[rows:], x, sems)
    z0, y0 = where[0], where[1]
    held[:rows] = own1[:, HD:]
    held[rows:] = own[:, HD:]
    for z in range(NZ):
        for c in (0, 1):
            block = (z * 8 + y0 * 2 + c - owner[z0]) & 63
            row = slot_of(block >> 1, z0, y0) * ROWS + (block & 1) * 8
            blocks[2 * z + c] = held[pl.ds(pl.multiple_of(row, 8), 8), :]


def spread_kernel(kv, out, sems):
    half = out.shape[-1]
    copies = [
        pltpu.make_async_copy(kv.at[:, pl.ds((i & 1) * half, half)], out.at[i], sems.at[i])
        for i in range(NY * 2)
    ]
    for copy in copies:
        copy.start()
    for copy in copies:
        copy.wait()


def join_kernel(one, two, *rest):
    batch, zero = rest[-2:]
    batch[:2] = one[...]
    batch[2:] = two[...]
    zero[0] = 0


def turn(v, cosine, sine):
    return v * cosine + pltpu.roll(v, HD // 2, 1) * sine


def decode_kernel(got, tables, out):
    for g in range(NZ):
        raw = (got[2 * g] + got[2 * g + 1]).astype(BF)
        out[g, :, :HD] = turn(
            raw[:, :HD].astype(F32), tables[g, :, :HD], tables[g, :, HD:]
        ).astype(BF)
        out[g, :, HD:] = raw[:, HD:]


def attend_kernel(where, own1, own2, got, cosine, sine, resident, out):
    z0, y0 = where[0], where[1]
    own = jnp.concatenate([own1[...], own2[...]])
    raw = (own[:, HD:] + got[:, HD:].astype(F32)).astype(BF)
    keys = turn(raw[:, :HD].astype(F32), cosine[...], sine[...]).astype(BF)
    q = own[:, :HD] + got[:, :HD].astype(F32)
    q = (turn(q, cosine[...], sine[...]) * HD ** (-0.5)).astype(BF)
    nt = (((1,), (1,)), ((), ()))
    old = lax.dot_general(q, resident[:, :HD], nt, preferred_element_type=F32)
    new = lax.dot_general(q, keys, nt, preferred_element_type=F32)
    token_q = tokens_of(lax.broadcasted_iota(jnp.int32, (TOKENS, 1), 0), z0, y0)
    token_k = tokens_of(lax.broadcasted_iota(jnp.int32, (1, TOKENS), 1), z0, y0)
    new = jnp.where(token_k <= token_q, new, masked_score)
    top = jnp.maximum(
        jnp.max(old, axis=1, keepdims=True), jnp.max(new, axis=1, keepdims=True)
    )
    old = jnp.exp(old - top)
    new = jnp.exp(new - top)
    total = jnp.sum(old, axis=1, keepdims=True) + jnp.sum(new, axis=1, keepdims=True)
    scale = 1.0 / total
    att = jnp.dot((old * scale).astype(BF), resident[:, HD:], preferred_element_type=F32)
    att = att + jnp.dot((new * scale).astype(BF), raw[:, HD:], preferred_element_type=F32)
    att = att.astype(BF)
    for slot in range(32):
        to = pl.multiple_of(place(slot, z0, y0) * ROWS, ROWS)
        out[pl.ds(to, ROWS), :] = att[slot * ROWS : (slot + 1) * ROWS]


VMEM = pl.BlockSpec(memory_space=pltpu.VMEM)
SMEM = pl.BlockSpec(memory_space=pltpu.SMEM)
HBM = pl.BlockSpec(memory_space=pltpu.HBM)


def call(kernel, shapes, specs, scratch=(), flops=0, moved=0, exps=0, limit=24, out=VMEM):
    return pl.pallas_call(
        kernel,
        out_shape=shapes,
        in_specs=specs,
        out_specs=jax.tree.map(lambda shape: SMEM if shape.shape == (1,) else out, shapes),
        scratch_shapes=scratch,
        compiler_params=pltpu.CompilerParams(vmem_limit_bytes=limit * 2**20),
        cost_estimate=pl.CostEstimate(flops=flops, bytes_accessed=moved, transcendentals=exps),
    )


def shaped(*shape, dtype=BF):
    return jax.ShapeDtypeStruct(shape, dtype)


def body(residual, norm_gain, query_weight, kv_weight, resident_cache, block_start, decode_owner):
    z0, y0, c0 = (lax.axis_index(a).astype(jnp.int32) for a in ("z", "y", "c"))
    width = residual.shape[2]
    half = width // 2
    where = jnp.stack([z0, y0, c0])

    widened = residual[0].astype(F32)
    scale_row = lax.rsqrt(jnp.mean(widened * widened, axis=-1, keepdims=True) + norm_eps)
    rows = (widened * scale_row).astype(BF)
    kept = lax.dynamic_slice_in_dim(rows, c0 * half, half, 1)
    crossed = lax.dynamic_slice_in_dim(rows, (1 - c0) * half, half, 1)
    sections = lax.axis_size("s")
    steps = [
        [
            ((s * NZ + z) * 2 + c, ((s + 1) % sections * NZ + (z ^ 4)) * 2 + (c ^ flip))
            for s in range(sections)
            for z in range(NZ)
            for c in (0, 1)
        ]
        for flip in (0, 1)
    ]
    same = lax.ppermute(kept, ("s", "z", "c"), steps[0])
    other = lax.ppermute(crossed, ("s", "z", "c"), steps[1])
    piece = jnp.where(c0 == 0, jnp.stack([same, other]), jnp.stack([other, same]))
    gain = lax.dynamic_slice_in_dim(norm_gain[0], c0 * half, half, 0)
    piece = (piece.reshape(ROWS, half).astype(F32) * gain[None]).astype(BF)

    arrived = (piece[0, 0] > 3e38).astype(jnp.int32)
    wq_other = swap_core(
        lax.dynamic_slice_in_dim(query_weight[0], (1 - c0) * half + arrived, half, 0)
    )
    kv_halves = call(spread_kernel, shaped(NY * 2, 32, half), [HBM], moved=2**22, limit=4,
        scratch=[pltpu.SemaphoreType.DMA((NY * 2,))], out=HBM)(kv_weight[0].T)
    wkv = lax.all_to_all(kv_halves, ("y", "c"), 0, 0).reshape(256, half)

    pair = jnp.stack([piece, across_z(piece, 4)])

    def join(one, two, *after):
        return call(
            join_kernel,
            (shaped(4, ROWS, half), shaped(1, dtype=jnp.int32)),
            [VMEM] * 2 + [HBM] * len(after),
            moved=2**20,
            limit=4,
        )(one, two, *after)

    batch1, late = join(pair, across_z(pair, 1), wq_other, wkv)

    def tables(tokens):
        angles = (block_start[0] + late[0] + tokens).astype(F32)[..., None] * frequencies(HD)
        cosine, sine = jnp.cos(angles), jnp.sin(angles)
        return jnp.concatenate([cosine, cosine], -1), jnp.concatenate([-sine, sine], -1)

    blocks = (z0 * 8 + y0 * 2 + c0 - decode_owner[0]) & 63
    decode_tokens = (blocks * 8)[:, None] + jnp.arange(8, dtype=jnp.int32)
    row_tokens = tokens_of(jnp.arange(TOKENS, dtype=jnp.int32), z0, y0)
    cosine, sine = tables(row_tokens)
    decode_tables = jnp.concatenate(tables(decode_tokens), -1)

    batch2, _ = join(across_z(pair, 2), across_z(pair, 3), cosine, sine, decode_tables)

    def everywhere(batch):
        after, before = along_y(batch, 1), along_y(batch, 3)
        return [batch, after, along_y(before[:2], 3), along_y(after[2:], 1), before]

    rows = TOKENS // 2
    projected = (shaped(rows, 3 * HD, dtype=F32), shaped(rows, 3 * HD))
    scratch = pltpu.VMEM((rows // ROWS, ROWS, half), BF)
    own1, send1, *weights = call(
        first_kernel,
        (*projected, shaped(half, 2 * HD), shaped(2 * HD, half)),
        [SMEM] + [HBM] * 8,
        scratch=[scratch, pltpu.SemaphoreType.DMA((8,))],
        flops=200 * rows * half * 512,
        moved=9 * 2**20,
    )(where, *everywhere(batch1), query_weight[0], wq_other, wkv)
    own2, send, blocks = call(
        second_kernel,
        (projected[0], shaped(TOKENS, 3 * HD), shaped(NZ * 2, 8, 2 * HD, dtype=F32)),
        [SMEM, SMEM] + [HBM] * 5 + [VMEM] * 4,
        scratch=[scratch, pltpu.VMEM((TOKENS, 2 * HD), F32), pltpu.SemaphoreType.DMA((5,))],
        flops=2 * rows * half * 512,
        moved=9 * 2**20,
    )(where, decode_owner[0], *everywhere(batch2), *weights, own1, send1)
    got = swap_core(send)
    blocks = lax.all_to_all(blocks, ("z", "c"), 0, 0)
    decode_kv = call(decode_kernel, shaped(NZ, 8, 2 * HD), [VMEM] * 2, moved=2**18, limit=4)(
        blocks, decode_tables
    )
    decode_kv = jnp.transpose(decode_kv, (1, 0, 2))[None]
    resident = lax.dynamic_index_in_dim(resident_cache[0], z0, 0, keepdims=False)
    attn = call(
        attend_kernel,
        shaped(TOKENS, HD),
        [SMEM] + [VMEM] * 6,
        flops=4 * TOKENS * 1024 * HD,
        moved=2**21,
        exps=TOKENS * 1024,
    )(where, own1, own2, got, cosine, sine, resident)
    return attn[None], decode_kv


def solution(mesh):
    sections = mesh.shape["section"]
    fine = Mesh(mesh.devices.reshape(sections, NZ, NY, 2), ("s", "z", "y", "c"))
    tp = ("z", "y", "c")
    return jax.shard_map(
        body,
        mesh=fine,
        in_specs=(
            P("s", tp, None),
            P("s", None),
            P("s", None, tp),
            P("s", None, tp),
            P("s", None, None, None),
            P("s"),
            P("s", None),
        ),
        out_specs=(P("s", None, tp), P("s", tp, None, None)),
        check_vma=False,
    )
```

```python
import math

import jax
import jax.numpy as jnp
from jax import lax
from jax.experimental import pallas as pl
from jax.experimental.pallas import tpu as pltpu
from jax.sharding import Mesh, PartitionSpec as P

BF = jnp.bfloat16
F32 = jnp.float32
rope_base = 500000.0
norm_eps = 1e-05
masked_score = -1e30

NZ, NY = 8, 4
ROWS = 16
TOKENS = 512
HD = 128


def frequencies(head_dim):
    half_dim = head_dim // 2
    base_freqs = jnp.exp(
        jnp.arange(half_dim, dtype=F32) * (-2.0 * math.log(rope_base) / head_dim)
    )
    wavelength = 2.0 * math.pi / base_freqs
    smooth = (8192.0 / wavelength - 1.0) / 3.0
    blended = (1.0 - smooth) * base_freqs / 8.0 + smooth * base_freqs
    return jnp.where(
        wavelength < 2048.0, base_freqs, jnp.where(wavelength > 8192.0, base_freqs / 8.0, blended)
    )


def along_y(value, k):
    return lax.ppermute(value, "y", [((i + k) % NY, i) for i in range(NY)])


def across_z(value, k):
    return lax.ppermute(value, "z", [(i, i ^ k) for i in range(NZ)])


def swap_core(value):
    return lax.ppermute(value, "c", [(0, 1), (1, 0)])


def place(slot, z0, y0):
    batch, k, i = slot >> 4, (slot >> 2) & 3, slot & 3
    z = z0 ^ (batch << 1) ^ (i >> 1) ^ (4 * (1 - (i & 1)))
    return (z << 2) | ((k + y0) & 3)


def slot_of(chip, z0, y0):
    far = (chip >> 2) ^ z0
    i = ((far & 1) << 1) | (1 - (far >> 2))
    return (((far >> 1) & 1) << 4) | (((chip - y0) & 3) << 2) | i


def tokens_of(row, z0, y0):
    return place(row >> 4, z0, y0) * ROWS + (row & 15)


PLACES = (0, 4, 8, 10, 12)


def project(pieces, early, late, wq, wkv, own, send, x, sems):
    early += [
        pltpu.make_async_copy(piece, x.at[at : at + piece.shape[0]], sems.at[i])
        for i, (piece, at) in enumerate(zip(pieces, PLACES))
    ]
    for copy in early + late:
        copy.start()
    for copy in early:
        copy.wait()
    rows = x[...].reshape(-1, x.shape[-1])
    kv = lax.dot_general(rows, wkv[...], (((1,), (1,)), ((), ())), preferred_element_type=F32)
    own[:, HD:] = kv
    send[:, HD:] = kv.astype(BF)
    for copy in late:
        copy.wait()
    q = jnp.dot(rows, wq[...], preferred_element_type=F32)
    own[:, :HD] = q[:, :HD]
    send[:, :HD] = q[:, HD:].astype(BF)


def first_kernel(where, *refs):
    *pieces, wq_mine, wq_other, wkv_far, own, send, wq, wkv, x, sems = refs
    half = x.shape[-1]
    rows = pl.ds(pl.multiple_of(where[2] * half, half), half)
    early = [pltpu.make_async_copy(wkv_far, wkv, sems.at[7])]
    late = [
        pltpu.make_async_copy(wq_mine.at[rows], wq.at[:, :HD], sems.at[5]),
        pltpu.make_async_copy(wq_other, wq.at[:, HD:], sems.at[6]),
    ]
    project(pieces, early, late, wq, wkv, own, send, x, sems)


def second_kernel(where, owner, *refs):
    pieces, (wq, wkv, own1, send1), (own, send, blocks, x, held, sems) = refs[:5], refs[5:9], refs[9:]
    rows = own.shape[0]
    send[:rows] = send1[...]
    project(pieces, [], [], wq, wkv, own, send.at[rows:], x, sems)
    z0, y0 = where[0], where[1]
    held[:rows] = own1[:, HD:]
    held[rows:] = own[:, HD:]
    for z in range(NZ):
        for c in (0, 1):
            block = (z * 8 + y0 * 2 + c - owner[z0]) & 63
            row = slot_of(block >> 1, z0, y0) * ROWS + (block & 1) * 8
            blocks[2 * z + c] = held[pl.ds(pl.multiple_of(row, 8), 8), :].astype(BF)


def spread_kernel(kv, out, sems):
    half = out.shape[-1]
    copies = [
        pltpu.make_async_copy(kv.at[:, pl.ds((i & 1) * half, half)], out.at[i], sems.at[i])
        for i in range(NY * 2)
    ]
    for copy in copies:
        copy.start()
    for copy in copies:
        copy.wait()


def join_kernel(one, two, *rest):
    batch, zero = rest[-2:]
    batch[:2] = one[...]
    batch[2:] = two[...]
    zero[0] = 0


def turn(v, cosine, sine):
    return v * cosine + pltpu.roll(v, HD // 2, 1) * sine


def decode_kernel(got, tables, out):
    for g in range(NZ):
        raw = (got[2 * g].astype(F32) + got[2 * g + 1].astype(F32)).astype(BF)
        out[g, :, :HD] = turn(
            raw[:, :HD].astype(F32), tables[g, :, :HD], tables[g, :, HD:]
        ).astype(BF)
        out[g, :, HD:] = raw[:, HD:]


def attend_kernel(where, own1, own2, got, cosine, sine, resident, out):
    z0, y0 = where[0], where[1]
    own = jnp.concatenate([own1[...], own2[...]])
    raw = (own[:, HD:] + got[:, HD:].astype(F32)).astype(BF)
    keys = turn(raw[:, :HD].astype(F32), cosine[...], sine[...]).astype(BF)
    q = own[:, :HD] + got[:, :HD].astype(F32)
    q = (turn(q, cosine[...], sine[...]) * HD ** (-0.5)).astype(BF)
    nt = (((1,), (1,)), ((), ()))
    old = lax.dot_general(q, resident[:, :HD], nt, preferred_element_type=F32)
    new = lax.dot_general(q, keys, nt, preferred_element_type=F32)
    token_q = tokens_of(lax.broadcasted_iota(jnp.int32, (TOKENS, 1), 0), z0, y0)
    token_k = tokens_of(lax.broadcasted_iota(jnp.int32, (1, TOKENS), 1), z0, y0)
    new = jnp.where(token_k <= token_q, new, masked_score)
    top = jnp.maximum(
        jnp.max(old, axis=1, keepdims=True), jnp.max(new, axis=1, keepdims=True)
    )
    old = jnp.exp(old - top)
    new = jnp.exp(new - top)
    total = jnp.sum(old, axis=1, keepdims=True) + jnp.sum(new, axis=1, keepdims=True)
    att = jnp.dot(old.astype(BF), resident[:, HD:], preferred_element_type=F32)
    att = att + jnp.dot(new.astype(BF), raw[:, HD:], preferred_element_type=F32)
    att = (att * (1.0 / total)).astype(BF)
    for slot in range(32):
        to = pl.multiple_of(place(slot, z0, y0) * ROWS, ROWS)
        out[pl.ds(to, ROWS), :] = att[slot * ROWS : (slot + 1) * ROWS]


VMEM = pl.BlockSpec(memory_space=pltpu.VMEM)
SMEM = pl.BlockSpec(memory_space=pltpu.SMEM)
HBM = pl.BlockSpec(memory_space=pltpu.HBM)


def call(kernel, shapes, specs, scratch=(), flops=0, moved=0, exps=0, limit=24, out=VMEM):
    return pl.pallas_call(
        kernel,
        out_shape=shapes,
        in_specs=specs,
        out_specs=jax.tree.map(lambda shape: SMEM if shape.shape == (1,) else out, shapes),
        scratch_shapes=scratch,
        compiler_params=pltpu.CompilerParams(vmem_limit_bytes=limit * 2**20),
        cost_estimate=pl.CostEstimate(flops=flops, bytes_accessed=moved, transcendentals=exps),
    )


def shaped(*shape, dtype=BF):
    return jax.ShapeDtypeStruct(shape, dtype)


def body(residual, norm_gain, query_weight, kv_weight, resident_cache, block_start, decode_owner):
    z0, y0, c0 = (lax.axis_index(a).astype(jnp.int32) for a in ("z", "y", "c"))
    width = residual.shape[2]
    half = width // 2
    where = jnp.stack([z0, y0, c0])

    widened = residual[0].astype(F32)
    scale_row = lax.rsqrt(jnp.mean(widened * widened, axis=-1, keepdims=True) + norm_eps)
    rows = (widened * scale_row).astype(BF)
    kept = lax.dynamic_slice_in_dim(rows, c0 * half, half, 1)
    crossed = lax.dynamic_slice_in_dim(rows, (1 - c0) * half, half, 1)
    sections = lax.axis_size("s")
    steps = [
        [
            ((s * NZ + z) * 2 + c, ((s + 1) % sections * NZ + (z ^ 4)) * 2 + (c ^ flip))
            for s in range(sections)
            for z in range(NZ)
            for c in (0, 1)
        ]
        for flip in (0, 1)
    ]
    same = lax.ppermute(kept, ("s", "z", "c"), steps[0])
    other = lax.ppermute(crossed, ("s", "z", "c"), steps[1])
    piece = jnp.where(c0 == 0, jnp.stack([same, other]), jnp.stack([other, same]))
    gain = lax.dynamic_slice_in_dim(norm_gain[0], c0 * half, half, 0)
    piece = (piece.reshape(ROWS, half).astype(F32) * gain[None]).astype(BF)

    arrived = (piece[0, 0] > 3e38).astype(jnp.int32)
    wq_other = swap_core(
        lax.dynamic_slice_in_dim(query_weight[0], (1 - c0) * half + arrived, half, 0)
    )
    kv_halves = call(spread_kernel, shaped(NY * 2, 32, half), [HBM], moved=2**22, limit=4,
        scratch=[pltpu.SemaphoreType.DMA((NY * 2,))], out=HBM)(kv_weight[0].T)
    wkv = lax.all_to_all(kv_halves, ("y", "c"), 0, 0).reshape(256, half)

    pair = jnp.stack([piece, across_z(piece, 4)])

    def join(one, two, *after):
        return call(
            join_kernel,
            (shaped(4, ROWS, half), shaped(1, dtype=jnp.int32)),
            [VMEM] * 2 + [HBM] * len(after),
            moved=2**20,
            limit=4,
        )(one, two, *after)

    batch1, late = join(pair, across_z(pair, 1), wq_other, wkv)

    def tables(tokens):
        angles = (block_start[0] + late[0] + tokens).astype(F32)[..., None] * frequencies(HD)
        cosine, sine = jnp.cos(angles), jnp.sin(angles)
        return jnp.concatenate([cosine, cosine], -1), jnp.concatenate([-sine, sine], -1)

    blocks = (z0 * 8 + y0 * 2 + c0 - decode_owner[0]) & 63
    decode_tokens = (blocks * 8)[:, None] + jnp.arange(8, dtype=jnp.int32)
    row_tokens = tokens_of(jnp.arange(TOKENS, dtype=jnp.int32), z0, y0)
    cosine, sine = tables(row_tokens)
    decode_tables = jnp.concatenate(tables(decode_tokens), -1)

    batch2, _ = join(across_z(pair, 2), across_z(pair, 3), cosine, sine, decode_tables)

    def everywhere(batch):
        after, before = along_y(batch, 1), along_y(batch, 3)
        return [batch, after, along_y(before[:2], 3), along_y(after[2:], 1), before]

    rows = TOKENS // 2
    projected = (shaped(rows, 3 * HD, dtype=F32), shaped(rows, 3 * HD))
    scratch = pltpu.VMEM((rows // ROWS, ROWS, half), BF)
    own1, send1, *weights = call(
        first_kernel,
        (*projected, shaped(half, 2 * HD), shaped(2 * HD, half)),
        [SMEM] + [HBM] * 8,
        scratch=[scratch, pltpu.SemaphoreType.DMA((8,))],
        flops=200 * rows * half * 512,
        moved=9 * 2**20,
    )(where, *everywhere(batch1), query_weight[0], wq_other, wkv)
    own2, send, blocks = call(
        second_kernel,
        (projected[0], shaped(TOKENS, 3 * HD), shaped(NZ * 2, 8, 2 * HD)),
        [SMEM, SMEM] + [HBM] * 5 + [VMEM] * 4,
        scratch=[scratch, pltpu.VMEM((TOKENS, 2 * HD), F32), pltpu.SemaphoreType.DMA((5,))],
        flops=2 * rows * half * 512,
        moved=9 * 2**20,
    )(where, decode_owner[0], *everywhere(batch2), *weights, own1, send1)
    got = swap_core(send)
    blocks = lax.all_to_all(blocks, ("z", "c"), 0, 0)
    decode_kv = call(decode_kernel, shaped(NZ, 8, 2 * HD), [VMEM] * 2, moved=2**18, limit=4)(
        blocks, decode_tables
    )
    decode_kv = jnp.transpose(decode_kv, (1, 0, 2))[None]
    resident = lax.dynamic_index_in_dim(resident_cache[0], z0, 0, keepdims=False)
    attn = call(
        attend_kernel,
        shaped(TOKENS, HD),
        [SMEM] + [VMEM] * 6,
        flops=4 * TOKENS * 1024 * HD,
        moved=2**21,
        exps=TOKENS * 1024,
    )(where, own1, own2, got, cosine, sine, resident)
    return attn[None], decode_kv


def solution(mesh):
    sections = mesh.shape["section"]
    fine = Mesh(mesh.devices.reshape(sections, NZ, NY, 2), ("s", "z", "y", "c"))
    tp = ("z", "y", "c")
    return jax.shard_map(
        body,
        mesh=fine,
        in_specs=(
            P("s", tp, None),
            P("s", None),
            P("s", None, tp),
            P("s", None, tp),
            P("s", None, None, None),
            P("s"),
            P("s", None),
        ),
        out_specs=(P("s", None, tp), P("s", tp, None, None)),
        check_vma=False,
    )
```

```python
import math

import jax
import jax.numpy as jnp
from jax import lax
from jax.experimental import pallas as pl
from jax.experimental.pallas import tpu as pltpu
from jax.sharding import Mesh, PartitionSpec as P

BF = jnp.bfloat16
F32 = jnp.float32
rope_base = 500000.0
norm_eps = 1e-05
masked_score = -1e30

NZ, NY = 8, 4
ROWS = 16
TOKENS = 512
HD = 128


def frequencies(head_dim):
    half_dim = head_dim // 2
    base_freqs = jnp.exp(
        jnp.arange(half_dim, dtype=F32) * (-2.0 * math.log(rope_base) / head_dim)
    )
    wavelength = 2.0 * math.pi / base_freqs
    smooth = (8192.0 / wavelength - 1.0) / 3.0
    blended = (1.0 - smooth) * base_freqs / 8.0 + smooth * base_freqs
    return jnp.where(
        wavelength < 2048.0, base_freqs, jnp.where(wavelength > 8192.0, base_freqs / 8.0, blended)
    )


def along_y(value, k):
    return lax.ppermute(value, "y", [((i + k) % NY, i) for i in range(NY)])


def across_z(value, k):
    return lax.ppermute(value, "z", [(i, i ^ k) for i in range(NZ)])


def swap_core(value):
    return lax.ppermute(value, "c", [(0, 1), (1, 0)])


def place(slot, z0, y0):
    batch, k, i = slot >> 4, (slot >> 2) & 3, slot & 3
    z = z0 ^ (batch << 1) ^ (i >> 1) ^ (4 * (1 - (i & 1)))
    return (z << 2) | ((k + y0) & 3)


def slot_of(chip, z0, y0):
    far = (chip >> 2) ^ z0
    i = ((far & 1) << 1) | (1 - (far >> 2))
    return (((far >> 1) & 1) << 4) | (((chip - y0) & 3) << 2) | i


def tokens_of(row, z0, y0):
    return place(row >> 4, z0, y0) * ROWS + (row & 15)


PLACES = (0, 4, 8, 10, 12)


def project(pieces, early, late, wq, wkv, own, send, x, sems):
    early += [
        pltpu.make_async_copy(piece, x.at[at : at + piece.shape[0]], sems.at[i])
        for i, (piece, at) in enumerate(zip(pieces, PLACES))
    ]
    for copy in early + late:
        copy.start()
    for copy in early:
        copy.wait()
    rows = x[...].reshape(-1, x.shape[-1])
    kv = lax.dot_general(rows, wkv[...], (((1,), (1,)), ((), ())), preferred_element_type=F32)
    own[:, HD:] = kv
    send[:, HD:] = kv.astype(BF)
    for copy in late:
        copy.wait()
    q = jnp.dot(rows, wq[...], preferred_element_type=F32)
    own[:, :HD] = q[:, :HD]
    send[:, :HD] = q[:, HD:].astype(BF)


def first_kernel(where, *refs):
    *pieces, wq_mine, wq_other, wkv_far, own, send, wq, wkv, x, sems = refs
    half = x.shape[-1]
    rows = pl.ds(pl.multiple_of(where[2] * half, half), half)
    early = [pltpu.make_async_copy(wkv_far, wkv, sems.at[7])]
    late = [
        pltpu.make_async_copy(wq_mine.at[rows], wq.at[:, :HD], sems.at[5]),
        pltpu.make_async_copy(wq_other, wq.at[:, HD:], sems.at[6]),
    ]
    project(pieces, early, late, wq, wkv, own, send, x, sems)


def second_kernel(where, owner, *refs):
    pieces, (wq, wkv, own1, send1), (own, send, blocks, x, held, sems) = refs[:5], refs[5:9], refs[9:]
    rows = own.shape[0]
    send[:rows] = send1[...]
    project(pieces, [], [], wq, wkv, own, send.at[rows:], x, sems)
    z0, y0 = where[0], where[1]
    held[:rows] = own1[:, HD:]
    held[rows:] = own[:, HD:]
    for z in range(NZ):
        for c in (0, 1):
            block = (z * 8 + y0 * 2 + c - owner[z0]) & 63
            row = slot_of(block >> 1, z0, y0) * ROWS + (block & 1) * 8
            blocks[2 * z + c] = held[pl.ds(pl.multiple_of(row, 8), 8), :].astype(BF)


def spread_kernel(kv, out, sems):
    half = out.shape[-1]
    copies = [
        pltpu.make_async_copy(kv.at[:, pl.ds((i & 1) * half, half)], out.at[i], sems.at[i])
        for i in range(NY * 2)
    ]
    for copy in copies:
        copy.start()
    for copy in copies:
        copy.wait()


def join_kernel(one, two, *rest):
    batch, zero = rest[-2:]
    batch[:2] = one[...]
    batch[2:] = two[...]
    zero[0] = 0


def turn(v, cosine, sine):
    return v * cosine + pltpu.roll(v, HD // 2, 1) * sine


def decode_kernel(_, got, tables, out):
    for g in range(NZ):
        raw = (got[2 * g].astype(F32) + got[2 * g + 1].astype(F32)).astype(BF)
        out[g, :, :HD] = turn(
            raw[:, :HD].astype(F32), tables[g, :, :HD], tables[g, :, HD:]
        ).astype(BF)
        out[g, :, HD:] = raw[:, HD:]


def attend_kernel(where, own1, own2, got, cosine, sine, resident, out, zero):
    zero[0] = 0
    z0, y0 = where[0], where[1]
    own = jnp.concatenate([own1[...], own2[...]])
    raw = (own[:, HD:] + got[:, HD:].astype(F32)).astype(BF)
    keys = turn(raw[:, :HD].astype(F32), cosine[...], sine[...]).astype(BF)
    q = own[:, :HD] + got[:, :HD].astype(F32)
    q = (turn(q, cosine[...], sine[...]) * HD ** (-0.5)).astype(BF)
    nt = (((1,), (1,)), ((), ()))
    old = lax.dot_general(q, resident[:, :HD], nt, preferred_element_type=F32)
    new = lax.dot_general(q, keys, nt, preferred_element_type=F32)
    token_q = tokens_of(lax.broadcasted_iota(jnp.int32, (TOKENS, 1), 0), z0, y0)
    token_k = tokens_of(lax.broadcasted_iota(jnp.int32, (1, TOKENS), 1), z0, y0)
    new = jnp.where(token_k <= token_q, new, masked_score)
    top = jnp.maximum(
        jnp.max(old, axis=1, keepdims=True), jnp.max(new, axis=1, keepdims=True)
    )
    old = jnp.exp(old - top)
    new = jnp.exp(new - top)
    total = jnp.sum(old, axis=1, keepdims=True) + jnp.sum(new, axis=1, keepdims=True)
    att = jnp.dot(old.astype(BF), resident[:, HD:], preferred_element_type=F32)
    att = att + jnp.dot(new.astype(BF), raw[:, HD:], preferred_element_type=F32)
    att = (att * (1.0 / total)).astype(BF)
    for slot in range(32):
        to = pl.multiple_of(place(slot, z0, y0) * ROWS, ROWS)
        out[pl.ds(to, ROWS), :] = att[slot * ROWS : (slot + 1) * ROWS]


VMEM = pl.BlockSpec(memory_space=pltpu.VMEM)
SMEM = pl.BlockSpec(memory_space=pltpu.SMEM)
HBM = pl.BlockSpec(memory_space=pltpu.HBM)


def call(kernel, shapes, specs, scratch=(), flops=0, moved=0, exps=0, limit=24, out=VMEM):
    return pl.pallas_call(
        kernel,
        out_shape=shapes,
        in_specs=specs,
        out_specs=jax.tree.map(lambda shape: SMEM if shape.shape == (1,) else out, shapes),
        scratch_shapes=scratch,
        compiler_params=pltpu.CompilerParams(vmem_limit_bytes=limit * 2**20),
        cost_estimate=pl.CostEstimate(flops=flops, bytes_accessed=moved, transcendentals=exps),
    )


def shaped(*shape, dtype=BF):
    return jax.ShapeDtypeStruct(shape, dtype)


def body(residual, norm_gain, query_weight, kv_weight, resident_cache, block_start, decode_owner):
    z0, y0, c0 = (lax.axis_index(a).astype(jnp.int32) for a in ("z", "y", "c"))
    width = residual.shape[2]
    half = width // 2
    where = jnp.stack([z0, y0, c0])

    widened = residual[0].astype(F32)
    scale_row = lax.rsqrt(jnp.mean(widened * widened, axis=-1, keepdims=True) + norm_eps)
    rows = (widened * scale_row).astype(BF)
    kept = lax.dynamic_slice_in_dim(rows, c0 * half, half, 1)
    crossed = lax.dynamic_slice_in_dim(rows, (1 - c0) * half, half, 1)
    sections = lax.axis_size("s")
    steps = [
        [
            ((s * NZ + z) * 2 + c, ((s + 1) % sections * NZ + (z ^ 4)) * 2 + (c ^ flip))
            for s in range(sections)
            for z in range(NZ)
            for c in (0, 1)
        ]
        for flip in (0, 1)
    ]
    same = lax.ppermute(kept, ("s", "z", "c"), steps[0])
    other = lax.ppermute(crossed, ("s", "z", "c"), steps[1])
    piece = jnp.where(c0 == 0, jnp.stack([same, other]), jnp.stack([other, same]))
    gain = lax.dynamic_slice_in_dim(norm_gain[0], c0 * half, half, 0)
    piece = (piece.reshape(ROWS, half).astype(F32) * gain[None]).astype(BF)

    arrived = (piece[0, 0] > 3e38).astype(jnp.int32)
    wq_other = swap_core(
        lax.dynamic_slice_in_dim(query_weight[0], (1 - c0) * half + arrived, half, 0)
    )
    kv_halves = call(spread_kernel, shaped(NY * 2, 32, half), [HBM], moved=2**22, limit=4,
        scratch=[pltpu.SemaphoreType.DMA((NY * 2,))], out=HBM)(kv_weight[0].T)
    wkv = lax.all_to_all(kv_halves, ("y", "c"), 0, 0).reshape(256, half)

    pair = jnp.stack([piece, across_z(piece, 4)])

    def join(one, two, *after):
        return call(
            join_kernel,
            (shaped(4, ROWS, half), shaped(1, dtype=jnp.int32)),
            [VMEM] * 2 + [HBM] * len(after),
            moved=2**20,
            limit=4,
        )(one, two, *after)

    batch1, late = join(pair, across_z(pair, 1), wq_other, wkv)

    def tables(tokens):
        angles = (block_start[0] + late[0] + tokens).astype(F32)[..., None] * frequencies(HD)
        cosine, sine = jnp.cos(angles), jnp.sin(angles)
        return jnp.concatenate([cosine, cosine], -1), jnp.concatenate([-sine, sine], -1)

    blocks = (z0 * 8 + y0 * 2 + c0 - decode_owner[0]) & 63
    decode_tokens = (blocks * 8)[:, None] + jnp.arange(8, dtype=jnp.int32)
    row_tokens = tokens_of(jnp.arange(TOKENS, dtype=jnp.int32), z0, y0)
    cosine, sine = tables(row_tokens)
    decode_tables = jnp.concatenate(tables(decode_tokens), -1)

    batch2, _ = join(across_z(pair, 2), across_z(pair, 3), cosine, sine, decode_tables)

    def everywhere(batch):
        after, before = along_y(batch, 1), along_y(batch, 3)
        return [batch, after, along_y(before[:2], 3), along_y(after[2:], 1), before]

    rows = TOKENS // 2
    projected = (shaped(rows, 3 * HD, dtype=F32), shaped(rows, 3 * HD))
    scratch = pltpu.VMEM((rows // ROWS, ROWS, half), BF)
    own1, send1, *weights = call(
        first_kernel,
        (*projected, shaped(half, 2 * HD), shaped(2 * HD, half)),
        [SMEM] + [HBM] * 8,
        scratch=[scratch, pltpu.SemaphoreType.DMA((8,))],
        flops=200 * rows * half * 512,
        moved=9 * 2**20,
    )(where, *everywhere(batch1), query_weight[0], wq_other, wkv)
    own2, send, blocks = call(
        second_kernel,
        (projected[0], shaped(TOKENS, 3 * HD), shaped(NZ * 2, 8, 2 * HD)),
        [SMEM, SMEM] + [HBM] * 5 + [VMEM] * 4,
        scratch=[scratch, pltpu.VMEM((TOKENS, 2 * HD), F32), pltpu.SemaphoreType.DMA((5,))],
        flops=2 * rows * half * 512,
        moved=9 * 2**20,
    )(where, decode_owner[0], *everywhere(batch2), *weights, own1, send1)
    got = swap_core(send)
    blocks = lax.all_to_all(blocks, ("z", "c"), 0, 0)
    resident = lax.dynamic_index_in_dim(resident_cache[0], z0, 0, keepdims=False)
    attn, done = call(
        attend_kernel,
        (shaped(TOKENS, HD), shaped(1, dtype=jnp.int32)),
        [SMEM] + [VMEM] * 6,
        flops=2**10,
        moved=2**10,
    )(where, own1, own2, got, cosine, sine, resident)
    decode_kv = call(decode_kernel, shaped(NZ, 8, 2 * HD), [SMEM] + [VMEM] * 2, moved=2**18, limit=4, flops=2**40)(
        done, blocks, decode_tables
    )
    decode_kv = jnp.transpose(decode_kv, (1, 0, 2))[None]
    return attn[None], decode_kv


def solution(mesh):
    sections = mesh.shape["section"]
    fine = Mesh(mesh.devices.reshape(sections, NZ, NY, 2), ("s", "z", "y", "c"))
    tp = ("z", "y", "c")
    return jax.shard_map(
        body,
        mesh=fine,
        in_specs=(
            P("s", tp, None),
            P("s", None),
            P("s", None, tp),
            P("s", None, tp),
            P("s", None, None, None),
            P("s"),
            P("s", None),
        ),
        out_specs=(P("s", None, tp), P("s", tp, None, None)),
        check_vma=False,
    )
```
